256 devices in a mesh: dp: 32 (over x, y, core), fsdp: 8 (over z).
Axes of the slice: x: 4, y: 4, z: 8, core: 2. Of those that a mesh axis runs over, the one named last changes fastest.
Arguments:
- patches: bfloat16 [131072, 1280], P(('dp', 'fsdp')), may hold values from -24 to 24
- patch_count: int32 [8192], P(('dp', 'fsdp')), may hold values from 1 to 16, as said below
- destination: int32 [8192], P(('dp', 'fsdp')), may hold values from 0 to 31, as said below
- qkv_weight: bfloat16 [1280, 1920], P('fsdp'), may hold values from -0.15625 to 0.15625
- qkv_bias: bfloat16 [1920], P('fsdp'), may hold values from -8 to 8
- norm_gain: bfloat16 [1280], P('fsdp'), may hold values from 0.099609375 to 1.8984375
- grad_out: bfloat16 [229376, 640], P(('dp', 'fsdp')), may hold values from -6 to 6
Outputs:
- attended: bfloat16 [229376, 640], P(('dp', 'fsdp'))
- grad_patches: bfloat16 [131072, 1280], P(('dp', 'fsdp'))
- grad_weight: float32 [1280, 1920], P('fsdp')
- grad_bias: float32 [1920], P('fsdp')
- grad_gain: float32 [1280], P('fsdp')
The draws below stay inside these ranges and needn't reach their ends.
Inputs may be any that keep to these rules, and one draw needn't show every extreme that they name: `destination`: the receiver of image i sits at the same index along fsdp as the device that holds it. Among one device's images at most 2 name the same receiver, and some device sends exactly 2 to one receiver; every device receives at most 56 images, and some device receives exactly 56. `patch_count`: every device holds an image with 16 real patches.
All inputs are finite; a program needn't handle non-finite values.
Results may differ from the reference program's by a relative error of at most 0.018.
The reference program's roundings to bfloat16 on the way count: a program that leaves them out, or rounds other values in their place, can miss the bound.
Values may be sent and summed in bfloat16 or wider, within the bound.
A program may use at most 128 MiB of HBM per device.

```python
import math
import jax
import jax.numpy as jnp
from jax import lax

D = 1280
HEADS = 8
HEAD_DIM = 80
SLOT = 16
IMG_DEV = 32
QKV = 1920
RECV_MAX = 56
IMAGES = 8192
RECV_ALL = 14336
N_DP = 32
N_FSDP = 8


def draw_destination(key, part):
    key = jax.random.fold_in(key, 11)
    quarter = N_DP // 4
    classes = jnp.array([0] * 14 + [1] * 10 + [2] * 4 + [3] * 4, dtype=jnp.int32)
    steps_in = jnp.array(list(range(14)) + list(range(10)) + list(range(4)) + list(range(4)), dtype=jnp.int32)

    def shuffle_one(mixer_key):
        return jax.random.permutation(mixer_key, IMG_DEV).astype(jnp.int32)

    def one_group(group_key):
        key_perm, key_base, key_mix = jax.random.split(group_key, 3)
        relabel = jax.random.permutation(key_perm, N_DP).astype(jnp.int32)
        base_shift = jax.random.randint(key_base, (4,), 0, quarter, dtype=jnp.int32)
        offsets = 4 * ((base_shift[classes] + steps_in) % quarter) + classes
        virtual = jnp.arange(N_DP, dtype=jnp.int32)
        landing = (4 * (virtual // 4))[:, None] + offsets[None, :]
        landing = relabel[landing % N_DP]
        shuffles = jax.vmap(shuffle_one)(jax.random.split(key_mix, N_DP))
        landing = jnp.take_along_axis(landing, shuffles, axis=1)
        inverse = jnp.argsort(relabel)
        return landing[inverse]
    groups = jax.vmap(one_group)(jax.random.split(key, N_FSDP))
    return jnp.transpose(groups, (1, 0, 2)).reshape(IMAGES).astype(jnp.int32)


def draw_patch_count(key, part):
    key = jax.random.fold_in(key, 5)
    key_base, key_full = jax.random.split(key)
    device_count = N_DP * N_FSDP
    base_counts = jax.random.randint(key_base, (device_count, IMG_DEV), 1, SLOT + 1, dtype=jnp.int32)
    full_pick = jax.random.randint(key_full, (device_count, 1), 0, IMG_DEV, dtype=jnp.int32)
    columns = jnp.arange(IMG_DEV, dtype=jnp.int32)[None, :]
    counts = jnp.where(columns == full_pick, SLOT, base_counts)
    return counts.reshape(IMAGES).astype(jnp.int32)


def draw_qkv_bias(key, part):
    key = jax.random.fold_in(key, 7)
    key_one = jax.random.fold_in(key, 0)
    drawn = jnp.clip(0.5 * jax.random.normal(key_one, (3 * HEADS * HEAD_DIM,)), -2.0, 2.0)
    return drawn.astype(jnp.float32).astype(jnp.bfloat16)


def with_spikes(drawn, rng, source, target, blocks, factor):
    def block_of(dim):
        return (jnp.arange(drawn.shape[dim]) // (drawn.shape[dim] // blocks)).reshape((-1,) + (1,) * (drawn.ndim - 1 - dim))

    near = jax.random.permutation(rng, blocks)[block_of(target)]
    second = (block_of(target) + blocks // 2) % blocks
    return jnp.where((block_of(source) == near) | (block_of(source) == second), factor * drawn, drawn)


def steps_of(rng, dims, cuts, low, top_value):
    level, own = 1.0, jax.random.fold_in(rng, 6)
    for axis_at, parts in cuts:
        heights = jnp.exp(jax.random.uniform(jax.random.fold_in(own, axis_at), (parts,), jnp.float32, low / len(cuts), top_value / len(cuts)))
        level = level * jnp.repeat(heights, dims[axis_at] // parts).reshape([-1 if axis == axis_at else 1 for axis in range(len(dims))])
    return level


def bell_draw(own_key, extent, scale, reach, shards=(), held_as=jnp.bfloat16):
    entries = scale * jax.random.normal(own_key, extent, jnp.float32)
    if shards:
        entries = entries * steps_of(own_key, extent, shards, -0.22, 0.18)
    return jnp.clip(entries, -reach, reach).astype(held_as)


def heavy_noise(rng, shape, spread, bound, shards, heavy, held_as=jnp.bfloat16):
    values = spread * jax.random.normal(rng, shape, jnp.float32)
    if shards:
        values = values * steps_of(rng, shape, shards, -0.22, 0.18)
    return jnp.clip(with_spikes(values, jax.random.fold_in(rng, 3), *heavy), -bound, bound).astype(held_as)


def setup_inputs(seed: int = 0) -> dict:
    keys = jax.random.split(jax.random.key(seed), 8)
    return {
        "patches": heavy_noise(keys[0], (IMAGES * SLOT, D), 1.0, 24.0, ((0, 256),), (0, 1, 256, 6.0)),
        "patch_count": draw_patch_count(jax.random.fold_in(keys[7], 71), 0),
        "destination": draw_destination(jax.random.fold_in(keys[7], 71), 0),
        "qkv_weight": bell_draw(keys[3], (D, QKV), D ** -0.5, 0.15625, ((0, 8),)),
        "qkv_bias": draw_qkv_bias(jax.random.fold_in(keys[7], 71), 0),
        "norm_gain": jnp.clip(1.0 + 0.18 * jax.random.normal(keys[5], (D,), jnp.float32), 0.099609375, 1.8984375).astype(jnp.bfloat16),
        "grad_out": bell_draw(keys[6], (RECV_ALL * SLOT, HEADS * HEAD_DIM), 1.0, 6.0, ((0, 256),)),
    }


def forward(block_images, counts, weight, bias_full, gain_full):
    batch, rows, model_width = block_images.shape
    rows_f32 = block_images.astype(jnp.float32)
    inverse_rms = lax.rsqrt(lax.optimization_barrier(jnp.mean(rows_f32 * rows_f32, axis=-1, keepdims=True)) + 1e-06)
    normed = (rows_f32 * inverse_rms * gain_full.astype(jnp.float32)).astype(jnp.bfloat16)
    normed_flat = normed.reshape(batch * rows, model_width)
    projected = jnp.dot(normed_flat, weight, preferred_element_type=jnp.float32) + bias_full.astype(jnp.float32)
    packed = projected.astype(jnp.bfloat16).reshape(batch, rows, 3, HEADS, HEAD_DIM)
    query = packed[:, :, 0]
    keyset = packed[:, :, 1]
    values = packed[:, :, 2]
    score_scale = 1.0 / math.sqrt(HEAD_DIM)
    scores = jnp.einsum('bqhe,bkhe->bhqk', query.astype(jnp.float32), keyset.astype(jnp.float32)) * score_scale
    slot_index = jnp.arange(rows, dtype=jnp.int32)
    key_valid = slot_index[None, :] < jnp.maximum(counts, 1)[:, None]
    scores = jnp.where(key_valid[:, None, None, :], scores, -1e+30)
    row_top = lax.optimization_barrier(jnp.max(scores, axis=-1, keepdims=True))
    exponent = jnp.exp(scores - row_top)
    attention = exponent / lax.optimization_barrier(jnp.sum(exponent, axis=-1, keepdims=True))
    attention_b = attention.astype(jnp.bfloat16)
    context = jnp.einsum('bhqk,bkhe->bqhe', attention_b.astype(jnp.float32), values.astype(jnp.float32))
    row_valid = slot_index[None, :] < counts[:, None]
    output = (context.reshape(batch, rows, HEADS * HEAD_DIM) * row_valid[:, :, None].astype(jnp.float32)).astype(jnp.bfloat16)
    kept_state = (rows_f32, inverse_rms, normed_flat, query, keyset, values, attention, attention_b, row_valid)
    return (output, kept_state)

def backward(kept_state, cotangent, weight, gain_full):
    rows_f32, inverse_rms, normed_flat, query, keyset, values, attention, attention_b, row_valid = kept_state
    batch, rows, model_width = rows_f32.shape
    score_scale = 1.0 / math.sqrt(HEAD_DIM)
    grad_rows = (cotangent * row_valid[:, :, None].astype(jnp.bfloat16)).reshape(batch, rows, HEADS, HEAD_DIM)
    grad_rows_f = grad_rows.astype(jnp.float32)
    d_values = jnp.einsum('bhqk,bqhe->bkhe', attention_b.astype(jnp.float32), grad_rows_f)
    d_attention = jnp.einsum('bqhe,bkhe->bhqk', grad_rows_f, values.astype(jnp.float32))
    d_scores = attention * (d_attention - lax.optimization_barrier(jnp.sum(d_attention * attention, axis=-1, keepdims=True))) * score_scale
    d_scores_b = d_scores.astype(jnp.bfloat16).astype(jnp.float32)
    d_query = jnp.einsum('bhqk,bkhe->bqhe', d_scores_b, keyset.astype(jnp.float32))
    d_keys = jnp.einsum('bhqk,bqhe->bkhe', d_scores_b, query.astype(jnp.float32))
    d_packed = jnp.stack([d_query, d_keys, d_values], axis=2).astype(jnp.bfloat16).reshape(batch * rows, 3 * HEADS * HEAD_DIM)
    d_weight = jnp.dot(normed_flat.T, d_packed, preferred_element_type=jnp.float32)
    d_bias = lax.optimization_barrier(jnp.sum(d_packed, axis=0, dtype=jnp.float32))
    d_normed = jnp.dot(d_packed, weight.T, preferred_element_type=jnp.float32).reshape(batch, rows, model_width)
    scaled = d_normed * gain_full.astype(jnp.float32)
    d_gain = lax.optimization_barrier(jnp.sum(d_normed * rows_f32 * inverse_rms, axis=(0, 1)))
    d_images = inverse_rms * scaled - rows_f32 * inverse_rms ** 3 * lax.optimization_barrier(jnp.mean(scaled * rows_f32, axis=-1, keepdims=True))
    return (d_images.astype(jnp.bfloat16), d_weight, d_bias, d_gain)

def reference(patches, patch_count, destination, qkv_weight, qkv_bias, norm_gain, grad_out):
    head_cols = HEADS * HEAD_DIM
    device_count = N_DP * N_FSDP
    image_index = jnp.arange(IMAGES, dtype=jnp.int32)
    fsdp_member = image_index // IMG_DEV % N_FSDP
    target = destination * N_FSDP + fsdp_member
    target_marks = (target[:, None] == jnp.arange(device_count, dtype=jnp.int32)[None, :]).astype(jnp.int32)
    earlier = jnp.cumsum(target_marks, axis=0) - target_marks
    slot_rank = lax.optimization_barrier(jnp.sum(earlier * target_marks, axis=1))
    slot_place = (target * RECV_MAX + slot_rank).astype(jnp.int32)
    cotangents = grad_out.reshape(RECV_ALL, SLOT, head_cols)[slot_place]
    all_images = patches.reshape(IMAGES, SLOT, D)
    block_size = 64
    block_count = IMAGES // block_size

    def visit_block(totals, block_index):
        first_image = (block_index * block_size).astype(jnp.int32)
        block_images = lax.dynamic_slice_in_dim(all_images, first_image, block_size, 0)
        block_counts = lax.dynamic_slice_in_dim(patch_count, first_image, block_size, 0)
        block_cots = lax.dynamic_slice_in_dim(cotangents, first_image, block_size, 0)
        block_output, kept_state = forward(block_images, block_counts, qkv_weight, qkv_bias, norm_gain)
        d_images, d_weight, d_bias, d_gain = backward(kept_state, block_cots, qkv_weight, norm_gain)
        return ((totals[0] + d_weight, totals[1] + d_bias, totals[2] + d_gain), (block_output, d_images))
    start_totals = (jnp.zeros((D, 3 * HEADS * HEAD_DIM), jnp.float32), jnp.zeros((3 * HEADS * HEAD_DIM,), jnp.float32), jnp.zeros((D,), jnp.float32))
    totals, stacked = lax.scan(visit_block, start_totals, jnp.arange(block_count, dtype=jnp.int32))
    outputs = stacked[0].reshape(IMAGES, SLOT, head_cols)
    grad_images = stacked[1].reshape(IMAGES * SLOT, D)
    attended = jnp.zeros((RECV_ALL, SLOT, head_cols), jnp.bfloat16).at[slot_place].set(outputs)
    grad_scale = 1.0 / math.sqrt(IMAGES * SLOT)
    return (attended.reshape(RECV_ALL * SLOT, head_cols), grad_images, totals[0] * grad_scale, totals[1] * grad_scale, totals[2] * grad_scale)
```

```python
import functools
import math

import jax
import jax.numpy as jnp
from jax import lax
from jax.experimental import pallas as pl
from jax.experimental.pallas import tpu as pltpu
from jax.sharding import PartitionSpec as P

MESH = pl.DeviceIdType.MESH
BF = jnp.bfloat16
F32 = jnp.float32
D = 1280
QKV = 1920
HEADS = 8
HD = 80
W3 = HEADS * HD
SLOT = 16
IMG = 32
ROWS = IMG * SLOT
RECV = 56
NDP = 32
NZ = 8
CHIPS = 16
SHARD = D // NZ
HALF = SHARD // 2
PIECES = 16
LIMIT = 58 * 2**20
COLS = ((0, 512), (512, 512), (1024, 512), (1536, 384))
VM = pl.BlockSpec(memory_space=pltpu.VMEM)
SM = pl.BlockSpec(memory_space=pltpu.SMEM)


def params(cid=None):
    if cid is None:
        return pltpu.CompilerParams(vmem_limit_bytes=LIMIT)
    return pltpu.CompilerParams(vmem_limit_bytes=LIMIT, collective_id=cid, has_side_effects=True)


def remote(src, dst, send, recv, where):
    return pltpu.make_async_remote_copy(
        src_ref=src, dst_ref=dst, send_sem=send, recv_sem=recv, device_id=where, device_id_type=MESH
    )


def table_kernel(dest_ref, lane_ref, cnt_ref, seen):
    def clear(e, _):
        seen[e] = 0
        return 0

    lax.fori_loop(0, NDP, clear, 0)

    def place(i, _):
        e = dest_ref[i]
        k = seen[e]
        lane_ref[i] = 2 * e + jnp.minimum(k, 1)
        seen[e] = k + 1
        return 0

    lax.fori_loop(0, IMG, place, 0)

    def spread(e, _):
        cnt_ref[e] = jnp.full((8, 128), seen[e], jnp.int32)
        return 0

    lax.fori_loop(0, NDP, spread, 0)


def tables(destination):
    return pl.pallas_call(
        table_kernel,
        out_shape=(
            jax.ShapeDtypeStruct((IMG,), jnp.int32),
            jax.ShapeDtypeStruct((NDP, 8, 128), jnp.int32),
        ),
        in_specs=[SM],
        out_specs=(SM, VM),
        scratch_shapes=[pltpu.SMEM((NDP,), jnp.int32)],
        compiler_params=params(),
    )(destination)


def gather_kernel(
    w_ref, small_ref, cnt_ref, grad_ref,
    wf_ref, params_ref, garr_ref, counts_ref,
    small_all, cbuf, stage, cvec, csm, starts,
    c_send, c_recv, g_send, g_recv, s_send, s_recv, r_send, r_recv, b_send, b_recv, l_sem,
):
    me = lax.axis_index("dp")
    z = lax.axis_index("fsdp")
    core = lax.rem(me, 2)
    sib = me + 1 - 2 * core

    barrier = pltpu.get_barrier_semaphore()

    def greet(k, _):
        pl.semaphore_signal(barrier, inc=1, device_id={"dp": lax.rem(me + k, NDP)}, device_id_type=MESH)
        return 0

    lax.fori_loop(1, NDP, greet, 0)
    for k in range(1, NZ):
        pl.semaphore_signal(barrier, inc=1, device_id={"fsdp": lax.rem(z + k, NZ)}, device_id_type=MESH)
    pl.semaphore_wait(barrier, NDP - 1 + NZ - 1)

    def count_copy(k):
        peer = lax.rem(me + k, NDP)
        return remote(cnt_ref.at[peer], cbuf.at[me], c_send.at[k], c_recv.at[me], {"dp": peer})

    def count_start(k, _):
        count_copy(k).start()
        return 0

    lax.fori_loop(1, NDP, count_start, 0)

    def rows_of(t):
        return pl.ds(pl.multiple_of(t * SHARD + core * HALF, 16), HALF)

    def ring_valid(d, s, q):
        return s < 3 or (s == 3 and (q < 2) == (d == 0))

    def ring_copy(d, s, q):
        cols = pl.ds(*COLS[q])
        if d == 0:
            t, to = lax.rem(z - s + NZ, NZ), lax.rem(z + 1, NZ)
        else:
            t, to = lax.rem(z + s, NZ), lax.rem(z + NZ - 1, NZ)
        dst = wf_ref.at[rows_of(t), cols]
        src = w_ref.at[pl.ds(pl.multiple_of(core * HALF, 16), HALF), cols] if s == 0 else dst
        return remote(src, dst, r_send.at[d, s, q], r_recv.at[d, s, q], {"fsdp": to})

    def arrived_from(d, s):
        return lax.rem(z - 1 - s + NZ, NZ) if d == 0 else lax.rem(z + 1 + s, NZ)

    def sib_copy(d, s, q):
        block = wf_ref.at[rows_of(arrived_from(d, s)), pl.ds(*COLS[q])]
        return remote(block, block, b_send.at[d, s, q], b_recv.at[d, s, q], {"dp": sib})

    for q in range(4):
        for d in range(2):
            ring_copy(d, 0, q).start()

    def small_copy(k):
        to = lax.rem(z + k, NZ)
        return remote(small_ref, small_all.at[z], s_send.at[k], s_recv.at[z], {"fsdp": to})

    for k in range(1, NZ):
        small_copy(k).start()
    small_all[z] = small_ref[...]
    wf_ref[pl.ds(pl.multiple_of(z * SHARD, 16), SHARD), :] = w_ref[...]

    cbuf[me] = cnt_ref[me]

    def count_wait(k, _):
        src = lax.rem(me + k, NDP)
        remote(cnt_ref.at[src], cbuf.at[src], c_send.at[k], c_recv.at[src], {"dp": src}).wait()
        return 0

    lax.fori_loop(1, NDP, count_wait, 0)
    lane = lax.broadcasted_iota(jnp.int32, (8, 128), 1)
    total = jnp.zeros((8, 128), jnp.int32)
    for s in range(NDP):
        total = total + jnp.where(lane == s, cbuf[s], 0)
    cvec[...] = total
    counts_ref[...] = total
    to_smem = pltpu.make_async_copy(cvec, csm, l_sem)
    to_smem.start()
    to_smem.wait()

    def prefix(s, start):
        starts[s] = start
        return start + csm[0, s]

    lax.fori_loop(0, NDP, prefix, jnp.int32(0))

    def grad_copy(k):
        peer = lax.rem(me + k, NDP)
        return remote(stage.at[peer], garr_ref.at[me], g_send.at[k], g_recv.at[me], {"dp": peer})

    def grad_start(k, _):
        peer = lax.rem(me + k, NDP)
        first = jnp.minimum(starts[peer], RECV - 1)
        second = jnp.minimum(first + 1, RECV - 1)
        stage[peer, 0] = grad_ref[first]
        stage[peer, 1] = grad_ref[second]
        grad_copy(k).start()
        return 0

    lax.fori_loop(1, NDP, grad_start, 0)
    first = jnp.minimum(starts[me], RECV - 1)
    garr_ref[me, 0] = grad_ref[first]
    garr_ref[me, 1] = grad_ref[jnp.minimum(first + 1, RECV - 1)]

    for s in range(4):
        for q in range(4):
            for d in range(2):
                if ring_valid(d, s, q):
                    ring_copy(d, s, q).wait_recv()
                    if ring_valid(d, s + 1, q):
                        ring_copy(d, s + 1, q).start()
                    sib_copy(d, s, q).start()

    for k in range(1, NZ):
        src = lax.rem(z + k, NZ)
        remote(small_ref, small_all.at[src], s_send.at[k], s_recv.at[src], {"fsdp": src}).wait()
    got = jnp.zeros((32, 128), F32)
    for s in range(NZ):
        got = got + small_all[s].astype(F32)
    params_ref[...] = got

    for s in range(4):
        for q in range(4):
            for d in range(2):
                if ring_valid(d, s, q):
                    ring_copy(d, s, q).wait_send()
                    sib_copy(d, s, q).wait()

    def grad_wait(k, _):
        src = lax.rem(me + k, NDP)
        remote(stage.at[src], garr_ref.at[src], g_send.at[k], g_recv.at[src], {"dp": src}).wait()
        return 0

    lax.fori_loop(1, NDP, grad_wait, 0)


def gather(weight, small, cnt, grad):
    dma = pltpu.SemaphoreType.DMA
    return pl.pallas_call(
        gather_kernel,
        out_shape=(
            jax.ShapeDtypeStruct((D, QKV), BF),
            jax.ShapeDtypeStruct((32, 128), F32),
            jax.ShapeDtypeStruct((NDP, 2, SLOT, W3), BF),
            jax.ShapeDtypeStruct((8, 128), jnp.int32),
        ),
        in_specs=[VM] * 4,
        out_specs=(VM,) * 4,
        scratch_shapes=[
            pltpu.VMEM((NZ, 32, 128), BF),
            pltpu.VMEM((NDP, 8, 128), jnp.int32),
            pltpu.VMEM((NDP, 2, SLOT, W3), BF),
            pltpu.VMEM((8, 128), jnp.int32),
            pltpu.SMEM((8, 128), jnp.int32),
            pltpu.SMEM((NDP,), jnp.int32),
            dma((NDP,)), dma((NDP,)), dma((NDP,)), dma((NDP,)), dma((NZ,)), dma((NZ,)),
            dma((2, 4, 4)), dma((2, 4, 4)), dma((2, 4, 4)), dma((2, 4, 4)), dma,
        ],
        compiler_params=params(1),
    )(weight, small, cnt, grad)


def dot_nn(a, b):
    return lax.dot_general(a, b, (((1,), (0,)), ((), ())), preferred_element_type=F32)


def dot_nt(a, b):
    return lax.dot_general(a, b, (((1,), (1,)), ((), ())), preferred_element_type=F32)


def window(h):
    low = (HD * h // 128) * 128
    high = -(-(HD * h + HD) // 128) * 128
    return low, high - low


def compute_kernel(
    lane_ref, x_ref, w_ref, par_ref, valid_ref, garr_ref,
    dx_ref, lanes_ref, p_ref,
    normed, normed_t, qkv, dqkv, g, att, dn, inv, row, dgain, small,
):
    for i in range(15):
        row[0:1, 128 * i : 128 * i + 128] = par_ref[i : i + 1, :]
    for i in range(10):
        row[1:2, 128 * i : 128 * i + 128] = par_ref[15 + i : 16 + i, :]

    def norm_block(b, _):
        rows = pl.ds(pl.multiple_of(b * 128, 128), 128)
        x = x_ref[rows, :].astype(F32)
        r = lax.rsqrt(jnp.mean(x * x, axis=-1, keepdims=True) + 1e-06)
        inv[rows, :] = jnp.broadcast_to(r, (128, 128))
        y = x * r * row[1:2, 0:D]
        normed[rows, :] = y.astype(BF)
        normed_t[:, rows] = y.T.astype(BF)
        return 0

    lax.fori_loop(0, 4, norm_block, 0)

    def project(n, _):
        cols = pl.ds(pl.multiple_of(n * 384, 128), 384)
        for m in range(2):
            r = dot_nn(normed[256 * m : 256 * m + 256, :], w_ref[:, cols]) + row[0:1, cols]
            qkv[256 * m : 256 * m + 256, cols] = r.astype(BF)
        return 0

    lax.fori_loop(0, 5, project, 0)

    def take_grad(i, _):
        g[pl.ds(pl.multiple_of(i * SLOT, SLOT), SLOT), :] = garr_ref[lane_ref[i]]
        return 0

    lax.fori_loop(0, IMG, take_grad, 0)

    dqkv[...] = jnp.zeros_like(dqkv)
    att[...] = jnp.zeros_like(att)
    scale = 1.0 / math.sqrt(HD)
    same = (
        lax.broadcasted_iota(jnp.int32, (128, 128), 0) // SLOT
        == lax.broadcasted_iota(jnp.int32, (128, 128), 1) // SLOT
    )

    def attend(b, _):
        rows = pl.ds(pl.multiple_of(b * 128, 128), 128)
        valid = jnp.broadcast_to(valid_ref[pl.ds(b, 1), :], (128, 128))
        keys = same & (valid > 0.5)
        live = valid.T
        for h in range(HEADS):
            low, width = window(h)
            col = lax.broadcasted_iota(jnp.int32, (128, width), 1) + low
            mine = (col >= HD * h) & (col < HD * h + HD)
            livew = live[:, :1] > 0.5
            zero = jnp.zeros((128, width), BF)
            q = jnp.where(mine, qkv[rows, low : low + width], zero)
            k = jnp.where(mine, qkv[rows, W3 + low : W3 + low + width], zero)
            v = jnp.where(mine, qkv[rows, 2 * W3 + low : 2 * W3 + low + width], zero)
            gh = jnp.where(mine & livew, g[rows, low : low + width], zero)
            s = jnp.where(keys, dot_nt(q, k) * scale, -1e30)
            e = jnp.exp(s - jnp.max(s, axis=-1, keepdims=True))
            p = e / jnp.sum(e, axis=-1, keepdims=True)
            o = jnp.where(livew, dot_nn(p.astype(BF), v), 0.0)
            dp = dot_nt(gh, v)
            ds = p * (dp - jnp.sum(dp * p, axis=-1, keepdims=True)) * scale
            dv = dot_nn(p.T.astype(BF), gh)
            dq = dot_nn(ds.astype(BF), k)
            dk = dot_nn(ds.T.astype(BF), q)
            att[rows, low : low + width] += o.astype(BF)
            dqkv[rows, low : low + width] += dq.astype(BF)
            dqkv[rows, W3 + low : W3 + low + width] += dk.astype(BF)
            dqkv[rows, 2 * W3 + low : 2 * W3 + low + width] += dv.astype(BF)
        return 0

    lax.fori_loop(0, 4, attend, 0)

    lanes_ref[...] = jnp.zeros_like(lanes_ref)

    def put_lane(i, _):
        lanes_ref[lane_ref[i]] = att[pl.ds(pl.multiple_of(i * SLOT, SLOT), SLOT), :]
        return 0

    lax.fori_loop(0, IMG, put_lane, 0)

    def weight_grad(j, _):
        left = normed_t[pl.ds(pl.multiple_of(j * 320, 64), 320), :]
        for k in range(3):
            r = dot_nn(left, dqkv[:, 640 * k : 640 * k + 640]).astype(BF)
            p_ref[pl.ds(4 * j, 4), 5 * k : 5 * k + 5] = r.reshape(4, 5, SLOT, 640)
        return 0

    lax.fori_loop(0, 4, weight_grad, 0)

    def input_grad(n, _):
        cols = pl.ds(pl.multiple_of(n * 256, 256), 256)
        for m in range(2):
            dn[256 * m : 256 * m + 256, cols] = dot_nt(dqkv[256 * m : 256 * m + 256, :], w_ref[cols, :])
        return 0

    lax.fori_loop(0, 5, input_grad, 0)

    dgain[...] = jnp.zeros_like(dgain)

    def finish(b, _):
        rows = pl.ds(pl.multiple_of(b * 32, 32), 32)
        x = x_ref[rows, :].astype(F32)
        r = inv[rows, 0:1]
        d = dn[rows, :]
        scaled = d * row[1:2, 0:D]
        m = jnp.mean(scaled * x, axis=-1, keepdims=True)
        dx_ref[rows, :] = (r * scaled - x * (r * r * r) * m).astype(BF)
        t = d * x * r
        dgain[:, 0:D] += t[0:8] + t[8:16] + t[16:24] + t[24:32]
        return 0

    lax.fori_loop(0, 16, finish, 0)

    def bias_sum(b, acc):
        t = dqkv[pl.ds(pl.multiple_of(b * 32, 32), 32), :].astype(F32)
        return acc + (t[0:8] + t[8:16] + t[16:24] + t[24:32])

    db = jnp.sum(lax.fori_loop(0, 16, bias_sum, jnp.zeros((8, QKV), F32)), axis=0, keepdims=True)
    dg = jnp.sum(dgain[:, 0:D], axis=0, keepdims=True)
    small[...] = jnp.zeros_like(small)
    for i in range(3):
        small[i : i + 1, :] = db[:, 640 * i : 640 * i + 640]
    for i in range(2):
        small[3 + i : 4 + i, :] = dg[:, 640 * i : 640 * i + 640]
    tile = small[...].astype(BF)
    for i in range(2 * NZ):
        p_ref[i, PIECES - 1] = tile


def compute(lane, x, weight, par, valid, garr):
    return pl.pallas_call(
        compute_kernel,
        out_shape=(
            jax.ShapeDtypeStruct((ROWS, D), BF),
            jax.ShapeDtypeStruct((2 * NDP, SLOT, W3), BF),
            jax.ShapeDtypeStruct((2 * NZ, PIECES, SLOT, 640), BF),
        ),
        in_specs=[SM] + [VM] * 5,
        out_specs=(VM,) * 3,
        scratch_shapes=[
            pltpu.VMEM((ROWS, D), BF),
            pltpu.VMEM((D, ROWS), BF),
            pltpu.VMEM((ROWS, QKV), BF),
            pltpu.VMEM((ROWS, QKV), BF),
            pltpu.VMEM((ROWS, W3), BF),
            pltpu.VMEM((ROWS, W3), BF),
            pltpu.VMEM((ROWS, D), F32),
            pltpu.VMEM((ROWS, 128), F32),
            pltpu.VMEM((8, QKV), F32),
            pltpu.VMEM((8, D), F32),
            pltpu.VMEM((16, 640), F32),
        ],
        compiler_params=params(),
    )(lane, x, weight, par, valid, garr)


def reduce_kernel(
    p_ref, lanes_ref,
    fin_ref, att_ref,
    pair, ring_in, ring_out, total, plane,
    a_send, a_recv, p_send, p_recv, r_send, r_recv, x_send, x_recv, y_send, y_recv, f_send, f_recv,
):
    me = lax.axis_index("dp")
    z = lax.axis_index("fsdp")
    core = lax.rem(me, 2)
    chip = me // 2
    sib = me + 1 - 2 * core
    ahead, behind = lax.rem(z + 1, NZ), lax.rem(z + NZ - 1, NZ)

    barrier = pltpu.get_barrier_semaphore()

    def greet(k, _):
        pl.semaphore_signal(barrier, inc=1, device_id={"dp": lax.rem(me + k, NDP)}, device_id_type=MESH)
        return 0

    lax.fori_loop(1, NDP, greet, 0)
    for to in (ahead, behind):
        pl.semaphore_signal(barrier, inc=1, device_id={"fsdp": to}, device_id_type=MESH)
    pl.semaphore_wait(barrier, NDP - 1 + 2)

    def target(off):
        return lax.rem(z + off + NZ, NZ)

    def pair_copy(off):
        t = target(off)
        return remote(p_ref.at[2 * t + 1 - core], pair.at[t], p_send.at[off + 3], p_recv.at[off + 3], {"dp": sib})

    for off in (4, 3, -3, 2, -2, 1, -1, 0):
        pair_copy(off).start()

    def att_copy(k):
        peer = lax.rem(me + k, NDP)
        return remote(lanes_ref.at[peer], att_ref.at[me], a_send.at[k], a_recv.at[me], {"dp": peer})

    def att_start(k, _):
        att_copy(k).start()
        return 0

    lax.fori_loop(1, NDP, att_start, 0)
    att_ref[me] = lanes_ref[me]

    def ring_valid(d, s, q):
        return s > 0 or (q < 2) == (d == 0)

    def ring_copy(d, s, q):
        part = pl.ds(4 * q, 4)
        return remote(
            ring_out.at[d, s, part], ring_in.at[d, s, part], r_send.at[d, s, q], r_recv.at[d, s, q],
            {"fsdp": behind if d else ahead},
        )

    def mine(off, q):
        t = target(off)
        part = pl.ds(4 * q, 4)
        return p_ref[2 * t + core, part].astype(F32) + pair[t, part].astype(F32)

    for s in range(4):
        for d in range(2):
            off = 4 - s if d == 0 else s - 4
            if s == 0:
                off = 4
            if s > 0 or d == 0:
                pair_copy(off).wait_recv()
        for q in range(4):
            for d in range(2):
                off = 4 - s if d == 0 else s - 4
                if s == 0:
                    off = 4
                if ring_valid(d, s, q):
                    r = mine(off, q)
                    if s > 0 and ring_valid(d, s - 1, q):
                        ring_copy(d, s - 1, q).wait_recv()
                        r = r + ring_in[d, s - 1, pl.ds(4 * q, 4)].astype(F32)
                    ring_out[d, s, pl.ds(4 * q, 4)] = r.astype(BF)
                    ring_copy(d, s, q).start()
    pair_copy(0).wait_recv()
    for q in range(4):
        r = mine(0, q)
        for d in range(2):
            ring_copy(d, 3, q).wait_recv()
            r = r + ring_in[d, 3, pl.ds(4 * q, 4)].astype(F32)
        total[pl.ds(4 * q, 4)] = r.astype(BF)

    def scatter_copy(k):
        i = lax.rem(chip + k, CHIPS)
        return remote(total.at[i], plane.at[chip], x_send.at[k], x_recv.at[chip], {"dp": 2 * i + core})

    def scatter_start(k, _):
        scatter_copy(k).start()
        return 0

    lax.fori_loop(1, CHIPS, scatter_start, 0)
    plane[chip] = total[chip]

    def scatter_wait(k, _):
        i = lax.rem(chip + k, CHIPS)
        remote(total.at[i], plane.at[i], x_send.at[k], x_recv.at[i], {"dp": 2 * i + core}).wait()
        return 0

    lax.fori_loop(1, CHIPS, scatter_wait, 0)
    r = jnp.zeros((SLOT, 640), F32)
    for i in range(CHIPS):
        r = r + plane[i].astype(F32)
    fin_ref[core, chip] = r.astype(BF)

    def share_copy(k, slot):
        i = lax.rem(chip + k, CHIPS)
        return remote(
            fin_ref.at[core, slot], fin_ref.at[core, slot], y_send.at[k], y_recv.at[slot], {"dp": 2 * i + core}
        )

    def share_start(k, _):
        share_copy(k, chip).start()
        return 0

    lax.fori_loop(1, CHIPS, share_start, 0)

    def share_wait(k, _):
        i = lax.rem(chip + k, CHIPS)
        share_copy(k, i).wait_recv()
        return 0

    lax.fori_loop(1, CHIPS, share_wait, 0)
    last = remote(fin_ref.at[core], fin_ref.at[core], f_send, f_recv, {"dp": sib})
    last.start()

    def share_sent(k, _):
        share_copy(k, chip).wait_send()
        return 0

    lax.fori_loop(1, CHIPS, share_sent, 0)
    for off in (4, 3, -3, 2, -2, 1, -1, 0):
        pair_copy(off).wait_send()
    for s in range(4):
        for q in range(4):
            for d in range(2):
                if ring_valid(d, s, q):
                    ring_copy(d, s, q).wait_send()

    def att_wait(k, _):
        src = lax.rem(me + k, NDP)
        remote(lanes_ref.at[src], att_ref.at[src], a_send.at[k], a_recv.at[src], {"dp": src}).wait()
        return 0

    lax.fori_loop(1, NDP, att_wait, 0)
    last.wait()


def reduce(pieces, lanes):
    dma = pltpu.SemaphoreType.DMA
    return pl.pallas_call(
        reduce_kernel,
        out_shape=(
            jax.ShapeDtypeStruct((2, PIECES, SLOT, 640), BF),
            jax.ShapeDtypeStruct((NDP, 2, SLOT, W3), BF),
        ),
        in_specs=[VM] * 2,
        out_specs=(VM,) * 2,
        scratch_shapes=[
            pltpu.VMEM((NZ, PIECES, SLOT, 640), BF),
            pltpu.VMEM((2, 4, PIECES, SLOT, 640), BF),
            pltpu.VMEM((2, 4, PIECES, SLOT, 640), BF),
            pltpu.VMEM((PIECES, SLOT, 640), BF),
            pltpu.VMEM((CHIPS, SLOT, 640), BF),
            dma((NDP,)), dma((NDP,)), dma((NZ,)), dma((NZ,)), dma((2, 4, 4)), dma((2, 4, 4)),
            dma((CHIPS,)), dma((CHIPS,)), dma((CHIPS,)), dma((CHIPS,)), dma, dma,
        ],
        compiler_params=params(2),
    )(pieces, lanes)


def finish_kernel(counts_ref, fin_ref, arr_ref, att_ref, gw_ref, small_ref):
    scale = 1.0 / math.sqrt(NDP * NZ * ROWS)
    att_ref[...] = jnp.zeros_like(att_ref)

    def place(src, start):
        n = counts_ref[0, src]
        for k in range(2):

            @pl.when(n > k)
            def _():
                att_ref[jnp.minimum(start + k, RECV - 1)] = arr_ref[2 * src + k]

        return start + n

    lax.fori_loop(0, NDP, place, jnp.int32(0))
    for c in range(2):
        for i in range(PIECES - 1):
            r0, c0 = HALF * c + SLOT * (i % 5), 640 * (i // 5)
            gw_ref[r0 : r0 + SLOT, c0 : c0 + 640] = fin_ref[c, i].astype(F32) * scale
    small_ref[...] = fin_ref[0, PIECES - 1].astype(F32) * scale


def finish(counts, fin, arr):
    return pl.pallas_call(
        finish_kernel,
        out_shape=(
            jax.ShapeDtypeStruct((RECV, SLOT, W3), BF),
            jax.ShapeDtypeStruct((SHARD, QKV), F32),
            jax.ShapeDtypeStruct((SLOT, 640), F32),
        ),
        in_specs=[SM, VM, VM],
        out_specs=(VM,) * 3,
        compiler_params=params(),
    )(counts, fin, arr)


def local(patches, patch_count, destination, qkv_weight, qkv_bias, norm_gain, grad_out):
    z = lax.axis_index("fsdp")
    small = jnp.zeros((4096,), BF)
    small = lax.dynamic_update_slice(small, qkv_bias, (z * (QKV // NZ),))
    small = lax.dynamic_update_slice(small, norm_gain, (QKV + z * SHARD,)).reshape(32, 128)
    valid = (jnp.arange(SLOT)[None, :] < jnp.maximum(patch_count, 1)[:, None]).astype(F32).reshape(4, 128)
    lane, cnt = tables(destination)
    weight, par, garr, counts = gather(qkv_weight, small, cnt, grad_out.reshape(RECV, SLOT, W3))
    dx, lanes, pieces = compute(lane, patches, weight, par, valid, garr.reshape(2 * NDP, SLOT, W3))
    fin, arr = reduce(pieces, lanes.reshape(NDP, 2, SLOT, W3))
    att, gw, sums = finish(counts, fin, arr.reshape(2 * NDP, SLOT, W3))
    gb = lax.dynamic_slice(sums[0:3].reshape(QKV), (z * (QKV // NZ),), (QKV // NZ,))
    gg = lax.dynamic_slice(sums[3:5].reshape(D), (z * SHARD,), (SHARD,))
    return att.reshape(RECV * SLOT, W3), dx, gw, gb, gg


def solution(mesh):
    return jax.shard_map(
        local,
        mesh=mesh,
        in_specs=(
            P(("dp", "fsdp"), None),
            P(("dp", "fsdp")),
            P(("dp", "fsdp")),
            P("fsdp", None),
            P("fsdp"),
            P("fsdp"),
            P(("dp", "fsdp"), None),
        ),
        out_specs=(
            P(("dp", "fsdp"), None),
            P(("dp", "fsdp"), None),
            P("fsdp", None),
            P("fsdp"),
            P("fsdp"),
        ),
        check_vma=False,
    )
```

```python
import functools
import math

import jax
import jax.numpy as jnp
from jax import lax
from jax.experimental import pallas as pl
from jax.experimental.pallas import tpu as pltpu
from jax.sharding import PartitionSpec as P

MESH = pl.DeviceIdType.MESH
BF = jnp.bfloat16
F32 = jnp.float32
D = 1280
QKV = 1920
HEADS = 8
HD = 80
W3 = HEADS * HD
SLOT = 16
IMG = 32
ROWS = IMG * SLOT
RECV = 56
NDP = 32
NZ = 8
CHIPS = 16
SHARD = D // NZ
HALF = SHARD // 2
PIECES = 16
LIMIT = 58 * 2**20
COLS = ((0, 512), (512, 512), (1024, 512), (1536, 384))
VM = pl.BlockSpec(memory_space=pltpu.VMEM)
SM = pl.BlockSpec(memory_space=pltpu.SMEM)


def params(cid=None):
    if cid is None:
        return pltpu.CompilerParams(vmem_limit_bytes=LIMIT)
    return pltpu.CompilerParams(vmem_limit_bytes=LIMIT, collective_id=cid, has_side_effects=True)


def remote(src, dst, send, recv, where):
    return pltpu.make_async_remote_copy(
        src_ref=src, dst_ref=dst, send_sem=send, recv_sem=recv, device_id=where, device_id_type=MESH
    )


def table_kernel(dest_ref, lane_ref, inverse_ref, cnt_ref, seen):
    def clear(e, _):
        seen[e] = 0
        return 0

    lax.fori_loop(0, NDP, clear, 0)

    def clear_lane(n, _):
        inverse_ref[n] = 0
        return 0

    lax.fori_loop(0, 2 * NDP, clear_lane, 0)

    def place(i, _):
        e = dest_ref[i]
        k = seen[e]
        lane_ref[i] = 2 * e + jnp.minimum(k, 1)
        inverse_ref[2 * e + jnp.minimum(k, 1)] = i
        seen[e] = k + 1
        return 0

    lax.fori_loop(0, IMG, place, 0)

    def spread(e, _):
        cnt_ref[e] = jnp.full((8, 128), seen[e], jnp.int32)
        return 0

    lax.fori_loop(0, NDP, spread, 0)


def tables(destination):
    return pl.pallas_call(
        table_kernel,
        out_shape=(
            jax.ShapeDtypeStruct((IMG,), jnp.int32),
            jax.ShapeDtypeStruct((2 * NDP,), jnp.int32),
            jax.ShapeDtypeStruct((NDP, 8, 128), jnp.int32),
        ),
        in_specs=[SM],
        out_specs=(SM, SM, VM),
        scratch_shapes=[pltpu.SMEM((NDP,), jnp.int32)],
        compiler_params=params(),
    )(destination)


def dot_nn(a, b):
    return lax.dot_general(a, b, (((1,), (0,)), ((), ())), preferred_element_type=F32)


def dot_nt(a, b):
    return lax.dot_general(a, b, (((1,), (1,)), ((), ())), preferred_element_type=F32)


def window(h):
    low = (HD * h // 128) * 128
    high = -(-(HD * h + HD) // 128) * 128
    return low, high - low


PARTS = ((0, 4), (4, 4), (8, 4), (12, 3))
ORDER = (4, 3, -3, 2, -2, 1, -1, 0)


def block_kernel(
    lane_ref, inverse_ref, x_ref, w_ref, small_ref, count_ref, live_ref, cnt_ref, grad_ref,
    dx_ref, fin_ref, arr_ref, counts_ref,
    wf, small_all, cbuf, stage, garr, cvec, csm, starts,
    normed, normed_t, qkv, dqkv, g, att, probs, dn, inv, row, dgain,
    lanes, p_all, pair, ring_in, ring_out, total, plane, sums, sums_all,
    c_send, c_recv, g_send, g_recv, s_send, s_recv, w_send, w_recv, b_send, b_recv, l_sem,
    a_send, a_recv, p_send, p_recv, r_send, r_recv, x_send, x_recv, y_send, y_recv, f_send, f_recv, z_send, z_recv,
):
    me = lax.axis_index("dp")
    z = lax.axis_index("fsdp")
    core = lax.rem(me, 2)
    chip = me // 2
    sib = me + 1 - 2 * core
    ahead, behind = lax.rem(z + 1, NZ), lax.rem(z + NZ - 1, NZ)

    barrier = pltpu.get_barrier_semaphore()

    def greet(k, _):
        pl.semaphore_signal(barrier, inc=1, device_id={"dp": lax.rem(me + k, NDP)}, device_id_type=MESH)
        return 0

    lax.fori_loop(1, NDP, greet, 0)
    for k in range(1, NZ):
        pl.semaphore_signal(barrier, inc=1, device_id={"fsdp": lax.rem(z + k, NZ)}, device_id_type=MESH)
    wf[pl.ds(pl.multiple_of(z * SHARD, 16), SHARD), :] = w_ref[...]
    cbuf[me] = cnt_ref[me]
    small_all[z] = small_ref[...]
    pl.semaphore_wait(barrier, NDP - 1 + NZ - 1)

    def count_copy(k, slot):
        peer = lax.rem(me + k, NDP)
        return remote(cnt_ref.at[peer], cbuf.at[slot], c_send.at[k], c_recv.at[slot], {"dp": peer})

    def count_start(k, _):
        count_copy(k, me).start()
        return 0

    lax.fori_loop(1, NDP, count_start, 0)

    def rows_of(t):
        return pl.ds(pl.multiple_of(t * SHARD + core * HALF, 16), HALF)

    def gather_valid(d, s, q):
        return s < 3 or (s == 3 and (q < 2) == (d == 0))

    def gather_copy(d, s, q):
        t = lax.rem(z - s + NZ, NZ) if d == 0 else lax.rem(z + s, NZ)
        block = wf.at[rows_of(t), pl.ds(*COLS[q])]
        return remote(block, block, w_send.at[d, s, q], w_recv.at[d, s, q], {"fsdp": behind if d else ahead})

    def sib_copy(d, s, q):
        t = lax.rem(z - 1 - s + NZ, NZ) if d == 0 else lax.rem(z + 1 + s, NZ)
        block = wf.at[rows_of(t), pl.ds(*COLS[q])]
        return remote(block, block, b_send.at[d, s, q], b_recv.at[d, s, q], {"dp": sib})

    def small_copy(k, slot):
        return remote(
            small_ref, small_all.at[slot], s_send.at[k], s_recv.at[slot], {"fsdp": lax.rem(z + k, NZ)}
        )

    for k in range(1, NZ):
        small_copy(k, z).start()
    for q in range(4):
        for d in range(2):
            gather_copy(d, 0, q).start()

    def count_wait(k, _):
        count_copy(k, lax.rem(me + k, NDP)).wait()
        return 0

    lax.fori_loop(1, NDP, count_wait, 0)
    lane = lax.broadcasted_iota(jnp.int32, (8, 128), 1)
    tally = jnp.zeros((8, 128), jnp.int32)
    for s in range(NDP):
        tally = tally + jnp.where(lane == s, cbuf[s], 0)
    cvec[...] = tally
    counts_ref[...] = tally
    to_smem = pltpu.make_async_copy(cvec, csm, l_sem)
    to_smem.start()
    to_smem.wait()

    def prefix(s, start):
        starts[s] = start
        return start + csm[0, s]

    lax.fori_loop(0, NDP, prefix, jnp.int32(0))

    def grad_copy(k, slot):
        peer = lax.rem(me + k, NDP)
        return remote(stage.at[peer], garr.at[slot], g_send.at[k], g_recv.at[slot], {"dp": peer})

    def pick_grad(peer):
        first = jnp.minimum(starts[peer], RECV - 1)
        return grad_ref[first], grad_ref[jnp.minimum(first + 1, RECV - 1)]

    def grad_start(k, _):
        peer = lax.rem(me + k, NDP)
        stage[peer, 0], stage[peer, 1] = pick_grad(peer)
        grad_copy(k, me).start()
        return 0

    lax.fori_loop(1, NDP, grad_start, 0)
    garr[me, 0], garr[me, 1] = pick_grad(me)

    for k in range(1, NZ):
        small_copy(k, lax.rem(z + k, NZ)).wait()
    got = jnp.zeros((32, 128), F32)
    for s in range(NZ):
        got = got + small_all[s].astype(F32)
    for i in range(15):
        row[0:1, 128 * i : 128 * i + 128] = got[i : i + 1, :]
    for i in range(10):
        row[1:2, 128 * i : 128 * i + 128] = got[15 + i : 16 + i, :]

    def norm_block(b, _):
        rows = pl.ds(pl.multiple_of(b * 128, 128), 128)
        x = x_ref[rows, :].astype(F32)
        r = lax.rsqrt(jnp.mean(x * x, axis=-1, keepdims=True) + 1e-06)
        inv[rows, :] = jnp.broadcast_to(r, (128, 128))
        y = x * r * row[1:2, 0:D]
        normed[rows, :] = y.astype(BF)
        normed_t[:, rows] = y.T.astype(BF)
        return 0

    lax.fori_loop(0, 4, norm_block, 0)

    for s in range(4):
        for q in range(4):
            for d in range(2):
                if gather_valid(d, s, q):
                    gather_copy(d, s, q).wait_recv()
                    if gather_valid(d, s + 1, q):
                        gather_copy(d, s + 1, q).start()
                    sib_copy(d, s, q).start()
    for s in range(4):
        for q in range(4):
            for d in range(2):
                if gather_valid(d, s, q):
                    sib_copy(d, s, q).wait_recv()

    def project(n, _):
        cols = pl.ds(pl.multiple_of(n * 384, 128), 384)
        for m in range(2):
            r = dot_nn(normed[256 * m : 256 * m + 256, :], wf[:, cols]) + row[0:1, cols]
            qkv[256 * m : 256 * m + 256, cols] = r.astype(BF)
        return 0

    lax.fori_loop(0, 5, project, 0)

    dqkv[...] = jnp.zeros_like(dqkv)
    att[...] = jnp.zeros_like(att)
    scale = 1.0 / math.sqrt(HD)
    image = lax.broadcasted_iota(jnp.int32, (SLOT, 128), 1) // SLOT
    key = lax.broadcasted_iota(jnp.int32, (SLOT, 128), 0)

    def compact(t):
        acc = jnp.where(image == 0, t[0:SLOT], 0.0)
        for i in range(1, 8):
            acc = jnp.where(image == i, t[SLOT * i : SLOT * i + SLOT], acc)
        return acc

    def spread(t):
        return jnp.concatenate([jnp.where(image == i, t, 0.0) for i in range(8)], axis=0)

    def own(h, t):
        low, width = window(h)
        col = lax.broadcasted_iota(jnp.int32, (128, width), 1) + low
        return jnp.where((col >= HD * h) & (col < HD * h + HD), t, jnp.zeros((128, width), BF))

    def head_cols(h, part):
        low, width = window(h)
        return slice(part * W3 + low, part * W3 + low + width)

    def live_rows(b):
        return jnp.broadcast_to(live_ref[pl.ds(b, 1), :], (128, 128)).T[:, :1] > 0.5

    def attend(b, _):
        rows = pl.ds(pl.multiple_of(b * 128, 128), 128)
        keys = key < jnp.maximum(jnp.broadcast_to(count_ref[pl.ds(b, 1), :], (SLOT, 128)), 1)
        live = live_rows(b)
        for h in range(HEADS):
            q = own(h, qkv[rows, head_cols(h, 0)])
            s = jnp.where(keys, compact(dot_nt(qkv[rows, head_cols(h, 1)], q)) * scale, -1e30)
            e = jnp.exp(s - jnp.max(s, axis=0, keepdims=True))
            probs[b, h] = e / jnp.sum(e, axis=0, keepdims=True)
        for h in range(HEADS):
            v = own(h, qkv[rows, head_cols(h, 2)])
            o = jnp.where(live, dot_nn(spread(probs[b, h]).T.astype(BF), v), 0.0)
            at = pl.ds(pl.multiple_of(8 * b, 8), 8), slice(None), head_cols(h, 0)
            att[at] += o.astype(BF).reshape(8, SLOT, -1)
        return 0

    lax.fori_loop(0, 4, attend, 0)

    def att_copy(k, slot):
        peer = lax.rem(me + k, NDP)
        return remote(lanes.at[peer], arr_ref.at[slot], a_send.at[k], a_recv.at[slot], {"dp": peer})

    def att_start(k, _):
        peer = lax.rem(me + k, NDP)
        lanes[peer, 0] = att[inverse_ref[2 * peer]]
        lanes[peer, 1] = att[inverse_ref[2 * peer + 1]]
        att_copy(k, me).start()
        return 0

    lax.fori_loop(1, NDP, att_start, 0)
    arr_ref[me, 0] = att[inverse_ref[2 * me]]
    arr_ref[me, 1] = att[inverse_ref[2 * me + 1]]

    def grad_wait(k, _):
        grad_copy(k, lax.rem(me + k, NDP)).wait()
        return 0

    lax.fori_loop(1, NDP, grad_wait, 0)

    def take_grad(i, _):
        n = lane_ref[i]
        g[i] = garr[n // 2, lax.rem(n, 2)]
        return 0

    lax.fori_loop(0, IMG, take_grad, 0)

    def attend_back(b, _):
        rows = pl.ds(pl.multiple_of(b * 128, 128), 128)
        live = live_rows(b)
        for h in range(HEADS):
            low, width = window(h)
            q, k, v = (own(h, qkv[rows, head_cols(h, i)]) for i in range(3))
            gh = g[pl.ds(pl.multiple_of(8 * b, 8), 8), :, low : low + width].reshape(128, width)
            gh = jnp.where(live, own(h, gh), jnp.zeros((128, width), BF))
            p = probs[b, h]
            dp = compact(dot_nt(v, gh))
            ds = spread(p * (dp - jnp.sum(dp * p, axis=0, keepdims=True)) * scale)
            dq = dot_nn(ds.T.astype(BF), k)
            dk = dot_nn(ds.astype(BF), q)
            dv = dot_nn(spread(p).astype(BF), gh)
            dqkv[rows, head_cols(h, 0)] += dq.astype(BF)
            dqkv[rows, head_cols(h, 1)] += dk.astype(BF)
            dqkv[rows, head_cols(h, 2)] += dv.astype(BF)
        return 0

    lax.fori_loop(0, 4, attend_back, 0)

    def target(off):
        return lax.rem(z + off + NZ, NZ)

    def pair_copy(off):
        t = target(off)
        return remote(p_all.at[2 * t + 1 - core], pair.at[t], p_send.at[off + 3], p_recv.at[off + 3], {"dp": sib})

    def weight_grad(off):
        t = target(off)
        left = normed_t[pl.ds(pl.multiple_of(t * SHARD, 32), SHARD), :]
        for k in range(3):
            r = dot_nn(left, dqkv[:, 640 * k : 640 * k + 640]).astype(BF)
            p_all[pl.ds(2 * t, 2), 5 * k : 5 * k + 5] = r.reshape(2, 5, SLOT, 640)
        pair_copy(off).start()

    def ring_valid(d, s, q):
        return s > 0 or (q < 2) == (d == 0)

    def ring_copy(d, s, q):
        part = pl.ds(*PARTS[q])
        return remote(
            ring_out.at[d, s, part], ring_in.at[d, s, part], r_send.at[d, s, q], r_recv.at[d, s, q],
            {"fsdp": behind if d else ahead},
        )

    def mine(off, q):
        t = target(off)
        part = pl.ds(*PARTS[q])
        return p_all[2 * t + core, part].astype(F32) + pair[t, part].astype(F32)

    def ring_step(d, s, q):
        if not ring_valid(d, s, q):
            return
        part = pl.ds(*PARTS[q])
        r = mine(4 if s == 0 else (s - 4 if d else 4 - s), q)
        if s > 0 and ring_valid(d, s - 1, q):
            ring_copy(d, s - 1, q).wait_recv()
            r = r + ring_in[d, s - 1, part].astype(F32)
        ring_out[d, s, part] = r.astype(BF)
        ring_copy(d, s, q).start()

    def input_grad(n):
        cols = slice(256 * n, 256 * n + 256)
        for m in range(2):
            dn[256 * m : 256 * m + 256, cols] = dot_nt(dqkv[256 * m : 256 * m + 256, :], wf[cols, :])

    def finish(b, _):
        rows = pl.ds(pl.multiple_of(b * 32, 32), 32)
        x = x_ref[rows, :].astype(F32)
        r = inv[rows, 0:1]
        d = dn[rows, :]
        scaled = d * row[1:2, 0:D]
        m = jnp.mean(scaled * x, axis=-1, keepdims=True)
        dx_ref[rows, :] = (r * scaled - x * (r * r * r) * m).astype(BF)
        t = d * x * r
        dgain[...] += t[0:8] + t[8:16] + t[16:24] + t[24:32]
        return 0

    def bias_sum(b, acc):
        t = dqkv[pl.ds(pl.multiple_of(b * 32, 32), 32), :].astype(F32)
        return acc + (t[0:8] + t[8:16] + t[16:24] + t[24:32])

    def sums_copy(k, slot):
        return remote(sums, sums_all.at[slot], z_send.at[k], z_recv.at[slot], {"fsdp": lax.rem(z + k, NZ)})

    def small_sums():
        db = jnp.sum(lax.fori_loop(0, 16, bias_sum, jnp.zeros((8, QKV), F32)), axis=0, keepdims=True)
        dg = jnp.sum(dgain[...], axis=0, keepdims=True)
        out = [db[:, 128 * i : 128 * i + 128] for i in range(15)] + [dg[:, 128 * i : 128 * i + 128] for i in range(10)]
        out = jnp.concatenate(out + [jnp.zeros((7, 128), F32)], axis=0)
        sums[...] = out.astype(BF)
        sums_all[z] = out.astype(BF)
        for k in range(1, NZ):
            sums_copy(k, z).start()

    weight_grad(4)
    weight_grad(3)
    weight_grad(-3)
    pair_copy(4).wait_recv()
    for q in range(4):
        for d in range(2):
            ring_step(d, 0, q)
    for off in ORDER[3:]:
        weight_grad(off)
    dgain[...] = jnp.zeros_like(dgain)
    beside = [functools.partial(input_grad, n) for n in range(5)]
    beside += [lambda n=n: lax.fori_loop(4 * n, 4 * n + 4, finish, 0) for n in range(4)] + [small_sums]
    for s in range(1, 4):
        for d in range(2):
            pair_copy(s - 4 if d else 4 - s).wait_recv()
        for q in range(4):
            for d in range(2):
                ring_step(d, s, q)
            if beside:
                beside.pop(0)()
    pair_copy(0).wait_recv()
    for q in range(4):
        part = pl.ds(*PARTS[q])
        r = mine(0, q)
        for d in range(2):
            ring_copy(d, 3, q).wait_recv()
            r = r + ring_in[d, 3, part].astype(F32)
        total[part] = r.astype(BF)
    for k in range(1, NZ):
        sums_copy(k, lax.rem(z + k, NZ)).wait()
    r = jnp.zeros((32, 128), F32)
    for s in range(NZ):
        r = r + sums_all[s].astype(F32)
    r = [jnp.concatenate([r[5 * i + j : 5 * i + j + 1, :] for j in range(5)], axis=1) for i in range(5)]
    total[PIECES - 1] = jnp.concatenate(r + [jnp.zeros((11, 640), F32)], axis=0).astype(BF)

    def scatter_copy(k):
        i = lax.rem(chip + k, CHIPS)
        return remote(total.at[i], plane.at[chip], x_send.at[k], x_recv.at[chip], {"dp": 2 * i + core})

    def scatter_start(k, _):
        scatter_copy(k).start()
        return 0

    lax.fori_loop(1, CHIPS, scatter_start, 0)
    plane[chip] = total[chip]

    def scatter_wait(k, _):
        i = lax.rem(chip + k, CHIPS)
        remote(total.at[i], plane.at[i], x_send.at[k], x_recv.at[i], {"dp": 2 * i + core}).wait()
        return 0

    lax.fori_loop(1, CHIPS, scatter_wait, 0)
    r = jnp.zeros((SLOT, 640), F32)
    for i in range(CHIPS):
        r = r + plane[i].astype(F32)
    fin_ref[core, chip] = r.astype(BF)

    def share_copy(k, slot):
        i = lax.rem(chip + k, CHIPS)
        return remote(
            fin_ref.at[core, slot], fin_ref.at[core, slot], y_send.at[k], y_recv.at[slot], {"dp": 2 * i + core}
        )

    def share_start(k, _):
        share_copy(k, chip).start()
        return 0

    lax.fori_loop(1, CHIPS, share_start, 0)

    def share_wait(k, _):
        i = lax.rem(chip + k, CHIPS)
        share_copy(k, i).wait_recv()
        return 0

    lax.fori_loop(1, CHIPS, share_wait, 0)
    last = remote(fin_ref.at[core], fin_ref.at[core], f_send, f_recv, {"dp": sib})
    last.start()

    def share_sent(k, _):
        share_copy(k, chip).wait_send()
        return 0

    lax.fori_loop(1, CHIPS, share_sent, 0)
    for off in ORDER:
        pair_copy(off).wait_send()
    for s in range(4):
        for q in range(4):
            for d in range(2):
                if ring_valid(d, s, q):
                    ring_copy(d, s, q).wait_send()
                if gather_valid(d, s, q):
                    gather_copy(d, s, q).wait_send()
                    sib_copy(d, s, q).wait_send()

    def att_wait(k, _):
        att_copy(k, lax.rem(me + k, NDP)).wait()
        return 0

    lax.fori_loop(1, NDP, att_wait, 0)
    last.wait()


def block(lane, inverse, x, weight, small, count, live, cnt, grad):
    dma = pltpu.SemaphoreType.DMA
    vmem = pltpu.VMEM
    return pl.pallas_call(
        block_kernel,
        out_shape=(
            jax.ShapeDtypeStruct((ROWS, D), BF),
            jax.ShapeDtypeStruct((2, PIECES, SLOT, 640), BF),
            jax.ShapeDtypeStruct((NDP, 2, SLOT, W3), BF),
            jax.ShapeDtypeStruct((8, 128), jnp.int32),
        ),
        in_specs=[SM] * 2 + [VM] * 7,
        out_specs=(VM,) * 4,
        scratch_shapes=[
            vmem((D, QKV), BF),
            vmem((NZ, 32, 128), BF),
            vmem((NDP, 8, 128), jnp.int32),
            vmem((NDP, 2, SLOT, W3), BF),
            vmem((NDP, 2, SLOT, W3), BF),
            vmem((8, 128), jnp.int32),
            pltpu.SMEM((8, 128), jnp.int32),
            pltpu.SMEM((NDP,), jnp.int32),
            vmem((ROWS, D), BF),
            vmem((D, ROWS), BF),
            vmem((ROWS, QKV), BF),
            vmem((ROWS, QKV), BF),
            vmem((IMG, SLOT, W3), BF),
            vmem((IMG, SLOT, W3), BF),
            vmem((4, HEADS, SLOT, 128), F32),
            vmem((ROWS, D), F32),
            vmem((ROWS, 128), F32),
            vmem((8, QKV), F32),
            vmem((8, D), F32),
            vmem((NDP, 2, SLOT, W3), BF),
            vmem((2 * NZ, PIECES - 1, SLOT, 640), BF),
            vmem((NZ, PIECES - 1, SLOT, 640), BF),
            vmem((2, 4, PIECES - 1, SLOT, 640), BF),
            vmem((2, 4, PIECES - 1, SLOT, 640), BF),
            vmem((PIECES, SLOT, 640), BF),
            vmem((CHIPS, SLOT, 640), BF),
            vmem((32, 128), BF),
            vmem((NZ, 32, 128), BF),
            dma((NDP,)), dma((NDP,)), dma((NDP,)), dma((NDP,)), dma((NZ,)), dma((NZ,)),
            dma((2, 4, 4)), dma((2, 4, 4)), dma((2, 4, 4)), dma((2, 4, 4)), dma,
            dma((NDP,)), dma((NDP,)), dma((NZ,)), dma((NZ,)), dma((2, 4, 4)), dma((2, 4, 4)),
            dma((CHIPS,)), dma((CHIPS,)), dma((CHIPS,)), dma((CHIPS,)), dma, dma, dma((NZ,)), dma((NZ,)),
        ],
        compiler_params=params(1),
    )(lane, inverse, x, weight, small, count, live, cnt, grad)


def finish_kernel(counts_ref, fin_ref, arr_ref, att_ref, gw_ref, small_ref):
    scale = 1.0 / math.sqrt(NDP * NZ * ROWS)
    att_ref[...] = jnp.zeros_like(att_ref)

    def place(src, start):
        n = counts_ref[0, src]
        for k in range(2):

            @pl.when(n > k)
            def _():
                att_ref[jnp.minimum(start + k, RECV - 1)] = arr_ref[2 * src + k]

        return start + n

    lax.fori_loop(0, NDP, place, jnp.int32(0))
    for c in range(2):
        for i in range(PIECES - 1):
            r0, c0 = HALF * c + SLOT * (i % 5), 640 * (i // 5)
            gw_ref[r0 : r0 + SLOT, c0 : c0 + 640] = fin_ref[c, i].astype(F32) * scale
    small_ref[...] = (fin_ref[0, PIECES - 1].astype(F32) + fin_ref[1, PIECES - 1].astype(F32)) * scale


def finish(counts, fin, arr):
    return pl.pallas_call(
        finish_kernel,
        out_shape=(
            jax.ShapeDtypeStruct((RECV, SLOT, W3), BF),
            jax.ShapeDtypeStruct((SHARD, QKV), F32),
            jax.ShapeDtypeStruct((SLOT, 640), F32),
        ),
        in_specs=[SM, VM, VM],
        out_specs=(VM,) * 3,
        compiler_params=params(),
    )(counts, fin, arr)


def local(patches, patch_count, destination, qkv_weight, qkv_bias, norm_gain, grad_out):
    z = lax.axis_index("fsdp")
    small = jnp.zeros((4096,), BF)
    small = lax.dynamic_update_slice(small, qkv_bias, (z * (QKV // NZ),))
    small = lax.dynamic_update_slice(small, norm_gain, (QKV + z * SHARD,)).reshape(32, 128)
    count = jnp.broadcast_to(patch_count[:, None], (IMG, SLOT)).reshape(4, 128)
    live = (jnp.arange(SLOT)[None, :] < patch_count[:, None]).astype(F32).reshape(4, 128)
    lane, inverse, cnt = tables(destination)
    dx, fin, arr, counts = block(
        lane, inverse, patches, qkv_weight, small, count, live, cnt, grad_out.reshape(RECV, SLOT, W3)
    )
    att, gw, sums = finish(counts, fin, arr.reshape(2 * NDP, SLOT, W3))
    gb = lax.dynamic_slice(sums[0:3].reshape(QKV), (z * (QKV // NZ),), (QKV // NZ,))
    gg = lax.dynamic_slice(sums[3:5].reshape(D), (z * SHARD,), (SHARD,))
    return att.reshape(RECV * SLOT, W3), dx, gw, gb, gg


def solution(mesh):
    return jax.shard_map(
        local,
        mesh=mesh,
        in_specs=(
            P(("dp", "fsdp"), None),
            P(("dp", "fsdp")),
            P(("dp", "fsdp")),
            P("fsdp", None),
            P("fsdp"),
            P("fsdp"),
            P(("dp", "fsdp"), None),
        ),
        out_specs=(
            P(("dp", "fsdp"), None),
            P(("dp", "fsdp"), None),
            P("fsdp", None),
            P("fsdp"),
            P("fsdp"),
        ),
        check_vma=False,
    )
```

```python
import functools
import math

import jax
import jax.numpy as jnp
from jax import lax
from jax.experimental import pallas as pl
from jax.experimental.pallas import tpu as pltpu
from jax.sharding import PartitionSpec as P

MESH = pl.DeviceIdType.MESH
BF = jnp.bfloat16
F32 = jnp.float32
D = 1280
QKV = 1920
HEADS = 8
HD = 80
W3 = HEADS * HD
SLOT = 16
IMG = 32
ROWS = IMG * SLOT
RECV = 56
NDP = 32
NZ = 8
CHIPS = 16
SHARD = D // NZ
HALF = SHARD // 2
PIECES = 16
LIMIT = 58 * 2**20
GET = ((0, 384), (640, 384), (1280, 384), (384, 256), (1024, 256), (1664, 256))
PUT = ((0, 256), (640, 256), (1280, 256), (256, 384), (896, 384), (1536, 384))
ORDER = (4, 3, -3, 2, -2, 1, -1, 0)
VM = pl.BlockSpec(memory_space=pltpu.VMEM)
SM = pl.BlockSpec(memory_space=pltpu.SMEM)
ANY = pl.BlockSpec(memory_space=pl.ANY)


def remote(src, dst, send, recv, where):
    return pltpu.make_async_remote_copy(
        src_ref=src, dst_ref=dst, send_sem=send, recv_sem=recv, device_id=where, device_id_type=MESH
    )


def dot_nn(a, b):
    return lax.dot_general(a, b, (((1,), (0,)), ((), ())), preferred_element_type=F32)


def dot_nt(a, b):
    return lax.dot_general(a, b, (((1,), (1,)), ((), ())), preferred_element_type=F32)


def window(h):
    low = (HD * h // 128) * 128
    high = -(-(HD * h + HD) // 128) * 128
    return low, high - low


def block_kernel(
    dest_ref, amount_ref, small_ref, x_hbm, w_hbm, grad_hbm,
    dx_hbm, att_hbm, gw_hbm, gb_ref, gg_ref,
    x_ref, grad_ref, dx_ref, out_ref, gw_ref,
    wf, small_all, cmine, cbuf, stage, garr, tabs, csm, lane_sm, inverse_sm, slot_sm, starts,
    normed, normed_t, qkv, dqkv, g, att, probs, dn, inv, row, dgain, count_v, live_v,
    lanes, arr, p_all, pair, ring_in, ring_out, tot, tot_small, plane0, plane1, fin0, fin1, sums, sums_all,
    l_sem, c_sem, g_sem, s_sem, a_sem, z_sem, x_sem, y_sem, f_sem, w_send, w_recv, b_send, b_recv,
    p_send, p_recv, r_send, r_recv,
):
    me = lax.axis_index("dp")
    z = lax.axis_index("fsdp")
    core = lax.rem(me, 2)
    chip = me // 2
    sib = me + 1 - 2 * core
    ahead, behind = lax.rem(z + 1, NZ), lax.rem(z + NZ - 1, NZ)
    plane, fin = (plane0, plane1), (fin0, fin1)

    def many(like, sems):
        return remote(like, like, sems.at[0], sems.at[1], {"dp": sib})

    x_in = pltpu.make_async_copy(x_hbm, x_ref, l_sem.at[0])
    w_in = pltpu.make_async_copy(w_hbm, wf.at[pl.ds(pl.multiple_of(z * SHARD, 32), SHARD), :], l_sem.at[1])
    grad_in = pltpu.make_async_copy(grad_hbm, grad_ref, l_sem.at[2])
    w_in.start()
    grad_in.start()
    x_in.start()

    barrier = pltpu.get_barrier_semaphore()

    def greet(k, _):
        pl.semaphore_signal(barrier, inc=1, device_id={"dp": lax.rem(me + k, NDP)}, device_id_type=MESH)
        return 0

    lax.fori_loop(1, NDP, greet, 0)
    for k in range(1, NZ):
        pl.semaphore_signal(barrier, inc=1, device_id={"fsdp": lax.rem(z + k, NZ)}, device_id_type=MESH)

    lane = lax.broadcasted_iota(jnp.int32, (1, 128), 1)
    dests = [dest_ref[i] for i in range(IMG)]
    per = jnp.zeros((1, 128), jnp.int32)
    to = jnp.zeros((1, 128), jnp.int32)
    for i in range(IMG):
        per = per + jnp.where(lane == dests[i], 1, 0)
        to = jnp.where(lane == i, dests[i], to)
    cmine[0] = per
    cbuf[me] = per
    rank = jnp.zeros((1, 128), jnp.int32)
    for i in range(IMG):
        rank = rank + jnp.where((to == dests[i]) & (lane > i), 1, 0)
    tabs[0] = 2 * to + jnp.minimum(rank, 1)
    lane_copy = pltpu.make_async_copy(tabs.at[pl.ds(0, 1)], lane_sm, l_sem.at[3])
    lane_copy.start()
    lane_copy.wait()
    source = jnp.zeros((1, 128), jnp.int32)
    for i in range(IMG):
        source = jnp.where(lane == lane_sm[0, 0, i], i, source)
    tabs[1] = source
    inverse_copy = pltpu.make_async_copy(tabs.at[pl.ds(1, 1)], inverse_sm, l_sem.at[4])
    inverse_copy.start()
    for b in range(4):
        have = jnp.zeros((1, 128), jnp.int32)
        for i in range(8):
            have = jnp.where(lane // SLOT == i, amount_ref[8 * b + i], have)
        count_v[b : b + 1, :] = have
        live_v[b : b + 1, :] = jnp.where(lax.rem(lane, SLOT) < have, 1.0, 0.0)
    small_all[z] = small_ref[...]
    w_in.wait()
    pl.semaphore_wait(barrier, NDP - 1 + NZ - 1)

    def rows_of(t):
        return pl.ds(pl.multiple_of(t * SHARD + core * HALF, 16), HALF)

    def gather_valid(d, s, q):
        return s < 3 or (s == 3 and (q in (0, 1, 3)) == (d == 0))

    def got_shard(d, s):
        return lax.rem(z - 1 - s + NZ, NZ) if d == 0 else lax.rem(z + 1 + s, NZ)

    def gather_copy(d, s, q):
        block = wf.at[rows_of(got_shard(d, s - 1)), pl.ds(*GET[q])]
        return remote(block, block, w_send, w_recv.at[d, s, q], {"fsdp": behind if d else ahead})

    def gather_start(h):
        for q in range(3 * h, 3 * h + 3):
            for d in range(2):
                gather_copy(d, 0, q).start()

    def gather_step(h, s):
        for q in range(3 * h, 3 * h + 3):
            for d in range(2):
                if not gather_valid(d, s, q):
                    continue
                gather_copy(d, s, q).wait_recv()
                if gather_valid(d, s + 1, q):
                    gather_copy(d, s + 1, q).start()
                block = wf.at[rows_of(got_shard(d, s)), pl.ds(*GET[q])]
                remote(block, block, b_send, b_recv.at[h], {"dp": sib}).start()

    def gather_end(h):
        like = wf.at[pl.ds(0, 7 * HALF), pl.ds(0, 768 if h else 1152)]
        remote(like, like, b_send, b_recv.at[h], {"dp": sib}).wait_recv()

    def count_start(k, _):
        remote(cmine.at[0], cbuf.at[me], c_sem.at[0], c_sem.at[1], {"dp": lax.rem(me + k, NDP)}).start()
        return 0

    gather_start(0)
    lax.fori_loop(1, NDP, count_start, 0)

    for k in range(1, NZ):
        remote(small_ref, small_all.at[z], s_sem.at[0], s_sem.at[1], {"fsdp": lax.rem(z + k, NZ)}).start()

    many(cbuf.at[pl.ds(0, NDP - 1)], c_sem).wait()
    to_smem = pltpu.make_async_copy(cbuf, csm, l_sem.at[3])
    to_smem.start()
    to_smem.wait()

    def prefix(s, carry):
        start, table = carry
        n = csm[s, 0, me]
        starts[s] = start
        table = jnp.where((lane >= start) & (lane < start + n), 2 * s + lane - start, table)
        return start + n, table

    _, table = lax.fori_loop(0, NDP, prefix, (jnp.int32(0), jnp.full((1, 128), -1, jnp.int32)))
    tabs[2] = table
    inverse_copy.wait()
    slot_copy = pltpu.make_async_copy(tabs.at[pl.ds(2, 1)], slot_sm, l_sem.at[4])
    slot_copy.start()

    def pick_grad(peer):
        first = jnp.minimum(starts[peer], RECV - 1)
        return grad_ref[first], grad_ref[jnp.minimum(first + 1, RECV - 1)]

    def grad_start(k, _):
        peer = lax.rem(me + k, NDP)
        stage[peer, 0], stage[peer, 1] = pick_grad(peer)
        remote(stage.at[peer], garr.at[me], g_sem.at[0], g_sem.at[1], {"dp": peer}).start()
        return 0

    grad_in.wait()
    gather_step(0, 0)
    lax.fori_loop(1, 16, grad_start, 0)
    gather_step(0, 1)
    lax.fori_loop(16, NDP, grad_start, 0)
    garr[me, 0], garr[me, 1] = pick_grad(me)

    many(small_all.at[pl.ds(0, NZ - 1)], s_sem).wait()
    for s in range(NZ):
        row[0:1, 240 * s : 240 * s + 240] = small_all[s, 0:1, 0:240]
        row[1:2, 160 * s : 160 * s + 160] = small_all[s, 1:2, 0:160]
    x_in.wait()

    def norm_block(b, _):
        rows = pl.ds(pl.multiple_of(b * 128, 128), 128)
        x = x_ref[rows, :].astype(F32)
        r = lax.rsqrt(jnp.mean(x * x, axis=-1, keepdims=True) + 1e-06)
        inv[rows, :] = jnp.broadcast_to(r, (128, 128))
        y = x * r * row[1:2, 0:D]
        normed[rows, :] = y.astype(BF)
        normed_t[:, rows] = y.T.astype(BF)
        return 0

    lax.fori_loop(0, 4, norm_block, 0)
    dqkv[...] = jnp.zeros_like(dqkv)
    att[...] = jnp.zeros_like(att)
    dgain[...] = jnp.zeros_like(dgain)

    def project(h):
        for low, width in GET[3 * h : 3 * h + 3]:
            for m in range(2):
                r = dot_nn(normed[256 * m : 256 * m + 256, :], wf[:, low : low + width]) + row[0:1, low : low + width]
                qkv[256 * m : 256 * m + 256, low : low + width] = r.astype(BF)

    scale = 1.0 / math.sqrt(HD)
    image = lax.broadcasted_iota(jnp.int32, (SLOT, 128), 1) // SLOT
    key = lax.broadcasted_iota(jnp.int32, (SLOT, 128), 0)

    def compact(t):
        acc = jnp.where(image == 0, t[0:SLOT], 0.0)
        for i in range(1, 8):
            acc = jnp.where(image == i, t[SLOT * i : SLOT * i + SLOT], acc)
        return acc

    def spread(t):
        return jnp.concatenate([jnp.where(image == i, t, 0.0) for i in range(8)], axis=0)

    def own(h, t):
        low, width = window(h)
        col = lax.broadcasted_iota(jnp.int32, (128, width), 1) + low
        return jnp.where((col >= HD * h) & (col < HD * h + HD), t, jnp.zeros((128, width), BF))

    def head_cols(h, part):
        low, width = window(h)
        return slice(part * W3 + low, part * W3 + low + width)

    def live_rows(b):
        return jnp.broadcast_to(live_v[pl.ds(b, 1), :], (128, 128)).T[:, :1] > 0.5

    def attend(heads, b, _):
        rows = pl.ds(pl.multiple_of(b * 128, 128), 128)
        keys = key < jnp.maximum(jnp.broadcast_to(count_v[pl.ds(b, 1), :], (SLOT, 128)), 1)
        live = live_rows(b)
        for h in heads:
            q = own(h, qkv[rows, head_cols(h, 0)])
            s = jnp.where(keys, compact(dot_nt(qkv[rows, head_cols(h, 1)], q)) * scale, -1e30)
            e = jnp.exp(s - jnp.max(s, axis=0, keepdims=True))
            probs[b, h] = e / jnp.sum(e, axis=0, keepdims=True)
        for h in heads:
            v = own(h, qkv[rows, head_cols(h, 2)])
            o = jnp.where(live, dot_nn(spread(probs[b, h]).T.astype(BF), v), 0.0)
            at = pl.ds(pl.multiple_of(8 * b, 8), 8), slice(None), head_cols(h, 0)
            att[at] += o.astype(BF).reshape(8, SLOT, -1)
        return 0

    def att_cols(h):
        return pl.ds(256, 384) if h else pl.ds(0, 256)

    def att_start(h, k, _):
        peer = lax.rem(me + k, NDP)
        cols = att_cols(h)
        for i in range(2):
            lanes[peer, i, :, cols] = att[inverse_sm[0, 0, 2 * peer + i], :, cols]
        src, dst = lanes.at[peer, :, :, cols], arr.at[me, :, :, cols]
        remote(src, dst, a_sem.at[h, 0], a_sem.at[h, 1], {"dp": peer}).start()
        return 0

    def att_send(h):
        lax.fori_loop(1, NDP, functools.partial(att_start, h), 0)
        cols = att_cols(h)
        for i in range(2):
            arr[me, i, :, cols] = att[inverse_sm[0, 0, 2 * me + i], :, cols]

    def take_grad(i, _):
        n = lane_sm[0, 0, i]
        g[i] = garr[n // 2, lax.rem(n, 2)]
        return 0

    def attend_back(heads, b, _):
        rows = pl.ds(pl.multiple_of(b * 128, 128), 128)
        live = live_rows(b)
        for h in heads:
            low, width = window(h)
            q, k, v = (own(h, qkv[rows, head_cols(h, i)]) for i in range(3))
            gh = g[pl.ds(pl.multiple_of(8 * b, 8), 8), :, low : low + width].reshape(128, width)
            gh = jnp.where(live, own(h, gh), jnp.zeros((128, width), BF))
            p = probs[b, h]
            dp = compact(dot_nt(v, gh))
            ds = spread(p * (dp - jnp.sum(dp * p, axis=0, keepdims=True)) * scale)
            dq = dot_nn(ds.T.astype(BF), k)
            dk = dot_nn(ds.astype(BF), q)
            dv = dot_nn(spread(p).astype(BF), gh)
            dqkv[rows, head_cols(h, 0)] += dq.astype(BF)
            dqkv[rows, head_cols(h, 1)] += dk.astype(BF)
            dqkv[rows, head_cols(h, 2)] += dv.astype(BF)
        return 0

    def target(off):
        return lax.rem(z + off + NZ, NZ)

    def weight_grad(h, *offs):
        for off in offs:
            t = target(off)
            left = normed_t[pl.ds(pl.multiple_of(t * SHARD, 32), SHARD), :]
            for low, width in PUT[3 * h : 3 * h + 3]:
                cols = pl.ds(low, width)
                p_all[t, :, :, cols] = dot_nn(left, dqkv[:, cols]).astype(BF).reshape(2, HALF, width)
                src, dst = p_all.at[t, 1 - core, :, cols], pair.at[t, :, cols]
                remote(src, dst, p_send, p_recv.at[h, off + 3], {"dp": sib}).start()

    def pair_wait(h, *offs):
        for off in offs:
            like = pair.at[target(off), :, pl.ds(0, 1152 if h else 768)]
            remote(like, like, p_send, p_recv.at[h, off + 3], {"dp": sib}).wait_recv()

    def ring_valid(d, s, q):
        return s > 0 or (q in (0, 1, 3)) == (d == 0)

    def ring_copy(d, s, q):
        cols = pl.ds(*PUT[q])
        return remote(
            ring_out.at[d, s, :, cols], ring_in.at[d, s, :, cols], r_send, r_recv.at[d, s, q],
            {"fsdp": behind if d else ahead},
        )

    def mine(off, q):
        t = target(off)
        cols = pl.ds(*PUT[q])
        return p_all[t, core, :, cols].astype(F32) + pair[t, :, cols].astype(F32)

    def ring_step(h, s):
        if s == 0:
            pair_wait(h, 4)
        else:
            pair_wait(h, 4 - s, s - 4)
        for q in range(3 * h, 3 * h + 3):
            for d in range(2):
                if not ring_valid(d, s, q):
                    continue
                cols = pl.ds(*PUT[q])
                r = mine(4 if s == 0 else (s - 4 if d else 4 - s), q)
                if s > 0 and ring_valid(d, s - 1, q):
                    ring_copy(d, s - 1, q).wait_recv()
                    r = r + ring_in[d, s - 1, :, cols].astype(F32)
                ring_out[d, s, :, cols] = r.astype(BF)
                ring_copy(d, s, q).start()

    def input_grad(n):
        cols = slice(256 * n, 256 * n + 256)
        for m in range(2):
            dn[256 * m : 256 * m + 256, cols] = dot_nt(dqkv[256 * m : 256 * m + 256, :], wf[cols, :])

    def finish(b, _):
        rows = pl.ds(pl.multiple_of(b * 32, 32), 32)
        x = x_ref[rows, :].astype(F32)
        r = inv[rows, 0:1]
        d = dn[rows, :]
        scaled = d * row[1:2, 0:D]
        m = jnp.mean(scaled * x, axis=-1, keepdims=True)
        dx_ref[rows, :] = (r * scaled - x * (r * r * r) * m).astype(BF)
        t = d * x * r
        dgain[...] += t[0:8] + t[8:16] + t[16:24] + t[24:32]
        return 0

    def bias_sum(b, acc):
        t = dqkv[pl.ds(pl.multiple_of(b * 32, 32), 32), :].astype(F32)
        return acc + (t[0:8] + t[8:16] + t[16:24] + t[24:32])

    dx_out = pltpu.make_async_copy(dx_ref, dx_hbm, l_sem.at[0])

    def small_sums():
        dx_out.start()
        db = jnp.sum(lax.fori_loop(0, 16, bias_sum, jnp.zeros((8, QKV), F32)), axis=0, keepdims=True)
        dg = jnp.sum(dgain[...], axis=0, keepdims=True)
        out = [db[:, 128 * i : 128 * i + 128] for i in range(15)] + [dg[:, 128 * i : 128 * i + 128] for i in range(10)]
        out = jnp.concatenate(out + [jnp.zeros((7, 128), F32)], axis=0)
        sums[...] = out.astype(BF)
        sums_all[z] = out.astype(BF)
        for k in range(1, NZ):
            remote(sums, sums_all.at[z], z_sem.at[0], z_sem.at[1], {"fsdp": lax.rem(z + k, NZ)}).start()

    def piece(h, i):
        return pl.ds(SLOT * (i % 5), SLOT), pl.ds(*PUT[3 * h + i // 5])

    def scatter(h, i):
        src = tot_small.at[:, pl.ds(0, 384 if h else 256)] if i == PIECES - 1 else tot.at[piece(h, i)]

        @pl.when(chip != i)
        def _():
            remote(src, plane[h].at[chip], x_sem.at[h, 0], x_sem.at[h, 1], {"dp": 2 * i + core}).start()

        @pl.when(chip == i)
        def _():
            plane[h][i] = src[...]

    def ring_end(h):
        pair_wait(h, 0)
        for q in range(3 * h, 3 * h + 3):
            cols = pl.ds(*PUT[q])
            r = mine(0, q)
            for d in range(2):
                ring_copy(d, 3, q).wait_recv()
                r = r + ring_in[d, 3, :, cols].astype(F32)
            tot[:, cols] = r.astype(BF)
            for i in range(5 * (q - 3 * h), 5 * (q - 3 * h) + 5):
                scatter(h, i)

    def plane_sum(h):
        many(plane[h].at[pl.ds(0, CHIPS - 1)], x_sem.at[h]).wait()
        r = plane[h][0].astype(F32)
        for i in range(1, CHIPS):
            r = r + plane[h][i].astype(F32)
        fin[h][core, chip] = r.astype(BF)
        block = fin[h].at[core, chip]

        def share_start(k, _):
            i = lax.rem(chip + k, CHIPS)
            remote(block, block, y_sem.at[h, 0], y_sem.at[h, 1], {"dp": 2 * i + core}).start()
            return 0

        lax.fori_loop(1, CHIPS, share_start, 0)

    def last_copy(h):
        return remote(fin[h].at[core], fin[h].at[core], f_sem.at[h, 0], f_sem.at[h, 1], {"dp": sib})

    def plane_end(h):
        many(fin[h].at[core, pl.ds(0, CHIPS - 1)], y_sem.at[h]).wait()
        last_copy(h).start()

    out_scale = 1.0 / math.sqrt(NDP * NZ * ROWS)

    def write_sums(h):
        last_copy(h).wait()
        for c in range(2):
            for i in range(PIECES - 1):
                rows, cols = piece(h, i)
                gw_ref[pl.ds(rows.start + HALF * c, SLOT), cols] = fin[h][c, i].astype(F32) * out_scale

    low_heads, high_heads = range(4), range(4, HEADS)
    gather_step(0, 2)
    gather_start(1)
    gather_step(0, 3)
    gather_end(0)
    project(0)
    gather_step(1, 0)
    lax.fori_loop(0, 4, functools.partial(attend, low_heads), 0)
    gather_step(1, 1)
    att_send(0)
    many(garr.at[pl.ds(0, NDP - 1)], g_sem).wait()
    lax.fori_loop(0, IMG, take_grad, 0)
    lax.fori_loop(0, 4, functools.partial(attend_back, low_heads), 0)
    gather_step(1, 2)
    weight_grad(0, 4, 3, -3)
    gather_step(1, 3)
    ring_step(0, 0)
    weight_grad(0, 2, -2, 1, -1, 0)
    gather_end(1)
    project(1)
    ring_step(0, 1)
    lax.fori_loop(0, 4, functools.partial(attend, high_heads), 0)
    ring_step(0, 2)
    lax.fori_loop(0, 4, functools.partial(attend_back, high_heads), 0)
    weight_grad(1, 4)
    ring_step(0, 3)
    weight_grad(1, 3, -3)
    ring_step(1, 0)
    att_send(1)
    weight_grad(1, 2, -2)
    ring_step(1, 1)
    weight_grad(1, 1, -1, 0)
    tot_small[...] = jnp.zeros_like(tot_small)
    scatter(0, PIECES - 1)
    ring_end(0)
    for n in range(3):
        input_grad(n)
    ring_step(1, 2)
    for n in range(3, 5):
        input_grad(n)
    lax.fori_loop(0, 8, finish, 0)
    ring_step(1, 3)
    lax.fori_loop(8, 16, finish, 0)
    small_sums()
    ring_end(1)
    plane_sum(0)
    many(sums_all.at[pl.ds(0, NZ - 1)], z_sem).wait()
    r = jnp.zeros((32, 128), F32)
    for s in range(NZ):
        r = r + sums_all[s].astype(F32)
    r = [jnp.concatenate([r[3 * i + j : 3 * i + j + 1, :] for j in range(3)], axis=1) for i in range(9)]
    tot_small[...] = jnp.concatenate(r + [jnp.zeros((7, 384), F32)], axis=0).astype(BF)
    scatter(1, PIECES - 1)

    for h in range(2):
        many(arr.at[pl.ds(0, NDP - 1), :, :, att_cols(h)], a_sem.at[h]).wait()
    slot_copy.wait()

    def place(i, _):
        n = slot_sm[0, 0, i]
        at = jnp.maximum(n, 0)
        block = arr[at // 2, lax.rem(at, 2)]
        out_ref[i] = jnp.where(n >= 0, block, jnp.zeros_like(block))
        return 0

    plane_sum(1)
    plane_end(0)
    lax.fori_loop(0, RECV, place, 0)
    att_out = pltpu.make_async_copy(out_ref, att_hbm, l_sem.at[1])
    att_out.start()
    write_sums(0)
    plane_end(1)
    write_sums(1)
    gw_out = pltpu.make_async_copy(gw_ref, gw_hbm, l_sem.at[2])
    gw_out.start()
    r = (fin1[0, PIECES - 1].astype(F32) + fin1[1, PIECES - 1].astype(F32)) * out_scale
    for i in range(25):
        part = r[i // 3 : i // 3 + 1, 128 * (i % 3) : 128 * (i % 3) + 128]
        if i < 15:
            row[2:3, 128 * i : 128 * i + 128] = part
        else:
            row[3:4, 128 * (i - 15) : 128 * (i - 15) + 128] = part
    gb = jnp.zeros((1, 240), F32)
    gg = jnp.zeros((1, 160), F32)
    for s in range(NZ):
        gb = jnp.where(z == s, row[2:3, 240 * s : 240 * s + 240], gb)
        gg = jnp.where(z == s, row[3:4, 160 * s : 160 * s + 160], gg)
    gb_ref[...] = gb
    gg_ref[...] = gg

    ring_like = wf.at[pl.ds(0, 560), :]
    pair_like = wf.at[pl.ds(0, 640), :]
    remote(ring_like, ring_like, w_send, w_recv.at[0, 0, 0], {"dp": sib}).wait_send()
    remote(ring_like, ring_like, b_send, b_recv.at[0], {"dp": sib}).wait_send()
    remote(ring_like, ring_like, r_send, r_recv.at[0, 0, 0], {"dp": sib}).wait_send()
    remote(pair_like, pair_like, p_send, p_recv.at[0, 0], {"dp": sib}).wait_send()
    dx_out.wait()
    att_out.wait()
    gw_out.wait()


def block(dest, amount, small, x, weight, grad):
    dma = pltpu.SemaphoreType.DMA
    vmem = pltpu.VMEM
    smem = pltpu.SMEM
    i32 = jnp.int32
    return pl.pallas_call(
        block_kernel,
        out_shape=(
            jax.ShapeDtypeStruct((ROWS, D), BF),
            jax.ShapeDtypeStruct((RECV, SLOT, W3), BF),
            jax.ShapeDtypeStruct((SHARD, QKV), F32),
            jax.ShapeDtypeStruct((1, 240), F32),
            jax.ShapeDtypeStruct((1, 160), F32),
        ),
        in_specs=[SM, SM, VM, ANY, ANY, ANY],
        out_specs=(ANY, ANY, ANY, VM, VM),
        scratch_shapes=[
            vmem((ROWS, D), BF),
            vmem((RECV, SLOT, W3), BF),
            vmem((ROWS, D), BF),
            vmem((RECV, SLOT, W3), BF),
            vmem((SHARD, QKV), F32),
            vmem((D, QKV), BF),
            vmem((NZ, 8, 256), F32),
            vmem((1, 1, 128), i32),
            vmem((NDP, 1, 128), i32),
            vmem((NDP, 2, SLOT, W3), BF),
            vmem((NDP, 2, SLOT, W3), BF),
            vmem((3, 1, 128), i32),
            smem((NDP, 1, 128), i32),
            smem((1, 1, 128), i32),
            smem((1, 1, 128), i32),
            smem((1, 1, 128), i32),
            smem((NDP,), i32),
            vmem((ROWS, D), BF),
            vmem((D, ROWS), BF),
            vmem((ROWS, QKV), BF),
            vmem((ROWS, QKV), BF),
            vmem((IMG, SLOT, W3), BF),
            vmem((IMG, SLOT, W3), BF),
            vmem((4, HEADS, SLOT, 128), F32),
            vmem((ROWS, D), F32),
            vmem((ROWS, 128), F32),
            vmem((8, QKV), F32),
            vmem((8, D), F32),
            vmem((8, 128), i32),
            vmem((8, 128), F32),
            vmem((NDP, 2, SLOT, W3), BF),
            vmem((NDP, 2, SLOT, W3), BF),
            vmem((NZ, 2, HALF, QKV), BF),
            vmem((NZ, HALF, QKV), BF),
            vmem((2, 4, HALF, QKV), BF),
            vmem((2, 4, HALF, QKV), BF),
            vmem((HALF, QKV), BF),
            vmem((SLOT, 384), BF),
            vmem((CHIPS, SLOT, 256), BF),
            vmem((CHIPS, SLOT, 384), BF),
            vmem((2, CHIPS, SLOT, 256), BF),
            vmem((2, CHIPS, SLOT, 384), BF),
            vmem((32, 128), BF),
            vmem((NZ, 32, 128), BF),
            dma((5,)),
            dma((2,)), dma((2,)), dma((2,)), dma((2, 2)), dma((2,)), dma((2, 2)), dma((2, 2)), dma((2, 2)),
            dma, dma((2, 4, 6)), dma, dma((2,)), dma, dma((2, 8)), dma, dma((2, 4, 6)),
        ],
        compiler_params=pltpu.CompilerParams(vmem_limit_bytes=LIMIT, collective_id=1, has_side_effects=True),
    )(dest, amount, small, x, weight, grad)


def hand_out_kernel(dx_in, att_in, gw_in, gb_in, gg_in, dx_out, att_out, gw_out, gb_out, gg_out, dx, att, gw, sems):
    steps = []
    for n, (src, mid, dst) in enumerate(((dx_in, dx, dx_out), (att_in, att, att_out), (gw_in, gw, gw_out))):
        size = src.shape[0] // 4
        for i in range(4):
            part = pl.ds(size * i, size)
            get = pltpu.make_async_copy(src.at[part], mid.at[part], sems.at[0, n, i])
            put = pltpu.make_async_copy(mid.at[part], dst.at[part], sems.at[1, n, i])
            get.start()
            steps.append((get, put))
    gb_out[...] = gb_in[...]
    gg_out[...] = gg_in[...]
    for get, put in steps:
        get.wait()
        put.start()
    for get, put in steps:
        put.wait()


def hand_out(*arrays):
    return pl.pallas_call(
        hand_out_kernel,
        out_shape=tuple(jax.ShapeDtypeStruct(a.shape, a.dtype) for a in arrays),
        in_specs=[ANY, ANY, ANY, VM, VM],
        out_specs=(ANY, ANY, ANY, VM, VM),
        scratch_shapes=[pltpu.VMEM(a.shape, a.dtype) for a in arrays[:3]] + [pltpu.SemaphoreType.DMA((2, 3, 4))],
        compiler_params=pltpu.CompilerParams(vmem_limit_bytes=LIMIT),
    )(*arrays)


def local(patches, patch_count, destination, qkv_weight, qkv_bias, norm_gain, grad_out):
    small = jnp.stack([jnp.pad(qkv_bias, (0, 16)), jnp.pad(norm_gain, (0, 96))]).astype(F32)
    small = jnp.pad(small, ((0, 6), (0, 0)))
    dx, att, gw, gb, gg = block(
        destination, patch_count, small, patches, qkv_weight, grad_out.reshape(RECV, SLOT, W3)
    )
    dx, att, gw, gb, gg = hand_out(dx, att, gw, gb, gg)
    return att.reshape(RECV * SLOT, W3), dx, gw, gb.reshape(-1), gg.reshape(-1)


def solution(mesh):
    return jax.shard_map(
        local,
        mesh=mesh,
        in_specs=(
            P(("dp", "fsdp"), None),
            P(("dp", "fsdp")),
            P(("dp", "fsdp")),
            P("fsdp", None),
            P("fsdp"),
            P("fsdp"),
            P(("dp", "fsdp"), None),
        ),
        out_specs=(
            P(("dp", "fsdp"), None),
            P(("dp", "fsdp"), None),
            P("fsdp", None),
            P("fsdp"),
            P("fsdp"),
        ),
        check_vma=False,
    )
```

```python
import functools
import math

import jax
import jax.numpy as jnp
from jax import lax
from jax.experimental import pallas as pl
from jax.experimental.pallas import tpu as pltpu
from jax.sharding import PartitionSpec as P

MESH = pl.DeviceIdType.MESH
BF = jnp.bfloat16
F32 = jnp.float32
D = 1280
QKV = 1920
HEADS = 8
HD = 80
W3 = HEADS * HD
SLOT = 16
IMG = 32
ROWS = IMG * SLOT
RECV = 56
NDP = 32
NZ = 8
CHIPS = 16
SHARD = D // NZ
HALF = SHARD // 2
PIECES = 16
LIMIT = 58 * 2**20
GET = ((0, 384), (640, 384), (1280, 384), (384, 256), (1024, 256), (1664, 256))
PUT = ((0, 256), (640, 256), (1280, 256), (256, 384), (896, 384), (1536, 384))
ORDER = (4, 3, -3, 2, -2, 1, -1, 0)
VM = pl.BlockSpec(memory_space=pltpu.VMEM)
SM = pl.BlockSpec(memory_space=pltpu.SMEM)
ANY = pl.BlockSpec(memory_space=pl.ANY)


def remote(src, dst, send, recv, where):
    return pltpu.make_async_remote_copy(
        src_ref=src, dst_ref=dst, send_sem=send, recv_sem=recv, device_id=where, device_id_type=MESH
    )


def dot_nn(a, b):
    return lax.dot_general(a, b, (((1,), (0,)), ((), ())), preferred_element_type=F32)


def dot_nt(a, b):
    return lax.dot_general(a, b, (((1,), (1,)), ((), ())), preferred_element_type=F32)


def window(h):
    low = (HD * h // 128) * 128
    high = -(-(HD * h + HD) // 128) * 128
    return low, high - low


def piece(h, i):
    return pl.ds(SLOT * (i % 5), SLOT), pl.ds(*PUT[3 * h + i // 5])


def block_kernel(
    dest_ref, amount_ref, bias_ref, gain_ref, x_hbm, w_hbm, grad_hbm,
    dx_hbm, att_hbm, fin0, fin1, gb_ref, gg_ref,
    x_ref, grad_ref, dx_ref, out_ref,
    wf, small_ref, small_all, cmine, cbuf, stage, garr, tabs, csm, lane_sm, inverse_sm, slot_sm, starts,
    normed, normed_t, qkv, dqkv, g, att, probs, dn, inv, row, dgain, count_v, live_v,
    lanes, arr, p_all, pair, ring_in, ring_out, tot, tot_small, plane0, plane1, sums, sums_all,
    l_sem, c_sem, g_sem, s_sem, a_sem, z_sem, x_sem, y_sem, f_sem, w_send, w_recv, b_send, b_recv,
    p_send, p_recv, r_send, r_recv,
):
    me = lax.axis_index("dp")
    z = lax.axis_index("fsdp")
    core = lax.rem(me, 2)
    chip = me // 2
    sib = me + 1 - 2 * core
    ahead, behind = lax.rem(z + 1, NZ), lax.rem(z + NZ - 1, NZ)
    plane, fin = (plane0, plane1), (fin0, fin1)

    def many(like, sems):
        return remote(like, like, sems.at[0], sems.at[1], {"dp": sib})

    x_in = pltpu.make_async_copy(x_hbm, x_ref, l_sem.at[0])
    w_in = pltpu.make_async_copy(w_hbm, wf.at[pl.ds(pl.multiple_of(z * SHARD, 32), SHARD), :], l_sem.at[1])
    grad_in = pltpu.make_async_copy(grad_hbm, grad_ref, l_sem.at[2])
    w_in.start()
    grad_in.start()
    x_in.start()

    barrier = pltpu.get_barrier_semaphore()

    def greet(k, _):
        pl.semaphore_signal(barrier, inc=1, device_id={"dp": lax.rem(me + k, NDP)}, device_id_type=MESH)
        return 0

    lax.fori_loop(1, NDP, greet, 0)
    for k in range(1, NZ):
        pl.semaphore_signal(barrier, inc=1, device_id={"fsdp": lax.rem(z + k, NZ)}, device_id_type=MESH)

    lane = lax.broadcasted_iota(jnp.int32, (1, 128), 1)
    dests = [dest_ref[i] for i in range(IMG)]
    per = jnp.zeros((1, 128), jnp.int32)
    to = jnp.zeros((1, 128), jnp.int32)
    for i in range(IMG):
        per = per + jnp.where(lane == dests[i], 1, 0)
        to = jnp.where(lane == i, dests[i], to)
    cmine[0] = per
    cbuf[me] = per
    rank = jnp.zeros((1, 128), jnp.int32)
    for i in range(IMG):
        rank = rank + jnp.where((to == dests[i]) & (lane > i), 1, 0)
    tabs[0] = 2 * to + jnp.minimum(rank, 1)
    lane_copy = pltpu.make_async_copy(tabs.at[pl.ds(0, 1)], lane_sm, l_sem.at[3])
    lane_copy.start()
    lane_copy.wait()
    source = jnp.zeros((1, 128), jnp.int32)
    for i in range(IMG):
        source = jnp.where(lane == lane_sm[0, 0, i], i, source)
    tabs[1] = source
    inverse_copy = pltpu.make_async_copy(tabs.at[pl.ds(1, 1)], inverse_sm, l_sem.at[4])
    inverse_copy.start()
    for b in range(4):
        have = jnp.zeros((1, 128), jnp.int32)
        for i in range(8):
            have = jnp.where(lane // SLOT == i, amount_ref[8 * b + i], have)
        count_v[b : b + 1, :] = have
        live_v[b : b + 1, :] = jnp.where(lax.rem(lane, SLOT) < have, 1.0, 0.0)
    small_ref[0:1, 0:240] = bias_ref[...].astype(F32).reshape(1, 240)
    small_ref[1:2, 0:160] = gain_ref[...].astype(F32).reshape(1, 160)
    small_all[z] = small_ref[...]
    w_in.wait()
    pl.semaphore_wait(barrier, NDP - 1 + NZ - 1)

    def rows_of(t):
        return pl.ds(pl.multiple_of(t * SHARD + core * HALF, 16), HALF)

    def gather_valid(d, s, q):
        return s < 3 or (s == 3 and (q in (0, 1, 3)) == (d == 0))

    def got_shard(d, s):
        return lax.rem(z - 1 - s + NZ, NZ) if d == 0 else lax.rem(z + 1 + s, NZ)

    def gather_copy(d, s, q):
        block = wf.at[rows_of(got_shard(d, s - 1)), pl.ds(*GET[q])]
        return remote(block, block, w_send, w_recv.at[d, s, q], {"fsdp": behind if d else ahead})

    def gather_start(h):
        for q in range(3 * h, 3 * h + 3):
            for d in range(2):
                gather_copy(d, 0, q).start()

    def gather_step(h, s):
        for q in range(3 * h, 3 * h + 3):
            for d in range(2):
                if not gather_valid(d, s, q):
                    continue
                gather_copy(d, s, q).wait_recv()
                if gather_valid(d, s + 1, q):
                    gather_copy(d, s + 1, q).start()
                block = wf.at[rows_of(got_shard(d, s)), pl.ds(*GET[q])]
                remote(block, block, b_send, b_recv.at[h], {"dp": sib}).start()

    def gather_end(h):
        like = wf.at[pl.ds(0, 7 * HALF), pl.ds(0, 768 if h else 1152)]
        remote(like, like, b_send, b_recv.at[h], {"dp": sib}).wait_recv()

    def count_start(k, _):
        remote(cmine.at[0], cbuf.at[me], c_sem.at[0], c_sem.at[1], {"dp": lax.rem(me + k, NDP)}).start()
        return 0

    gather_start(0)
    gather_start(1)
    lax.fori_loop(1, NDP, count_start, 0)

    for k in range(1, NZ):
        remote(small_ref, small_all.at[z], s_sem.at[0], s_sem.at[1], {"fsdp": lax.rem(z + k, NZ)}).start()

    many(cbuf.at[pl.ds(0, NDP - 1)], c_sem).wait()
    to_smem = pltpu.make_async_copy(cbuf, csm, l_sem.at[3])
    to_smem.start()
    to_smem.wait()

    def prefix(s, carry):
        start, table = carry
        n = csm[s, 0, me]
        starts[s] = start
        table = jnp.where((lane >= start) & (lane < start + n), 2 * s + lane - start, table)
        return start + n, table

    _, table = lax.fori_loop(0, NDP, prefix, (jnp.int32(0), jnp.full((1, 128), -1, jnp.int32)))
    tabs[2] = table
    inverse_copy.wait()
    slot_copy = pltpu.make_async_copy(tabs.at[pl.ds(2, 1)], slot_sm, l_sem.at[4])
    slot_copy.start()

    def pick_grad(peer):
        first = jnp.minimum(starts[peer], RECV - 1)
        return grad_ref[first], grad_ref[jnp.minimum(first + 1, RECV - 1)]

    def grad_start(k, _):
        peer = lax.rem(me + k, NDP)
        stage[peer, 0], stage[peer, 1] = pick_grad(peer)
        remote(stage.at[peer], garr.at[me], g_sem.at[0], g_sem.at[1], {"dp": peer}).start()
        return 0

    grad_in.wait()
    gather_step(0, 0)
    gather_step(1, 0)
    lax.fori_loop(1, 16, grad_start, 0)
    gather_step(0, 1)
    gather_step(1, 1)
    lax.fori_loop(16, NDP, grad_start, 0)
    garr[me, 0], garr[me, 1] = pick_grad(me)

    many(small_all.at[pl.ds(0, NZ - 1)], s_sem).wait()
    for s in range(NZ):
        row[0:1, 240 * s : 240 * s + 240] = small_all[s, 0:1, 0:240]
        row[1:2, 160 * s : 160 * s + 160] = small_all[s, 1:2, 0:160]
    x_in.wait()

    def norm_block(b, _):
        rows = pl.ds(pl.multiple_of(b * 128, 128), 128)
        x = x_ref[rows, :].astype(F32)
        r = lax.rsqrt(jnp.mean(x * x, axis=-1, keepdims=True) + 1e-06)
        inv[rows, :] = jnp.broadcast_to(r, (128, 128))
        y = x * r * row[1:2, 0:D]
        normed[rows, :] = y.astype(BF)
        normed_t[:, rows] = y.T.astype(BF)
        return 0

    lax.fori_loop(0, 4, norm_block, 0)
    dqkv[...] = jnp.zeros_like(dqkv)
    att[...] = jnp.zeros_like(att)
    dgain[...] = jnp.zeros_like(dgain)

    def project(h):
        for low, width in GET[3 * h : 3 * h + 3]:
            for m in range(2):
                r = dot_nn(normed[256 * m : 256 * m + 256, :], wf[:, low : low + width]) + row[0:1, low : low + width]
                qkv[256 * m : 256 * m + 256, low : low + width] = r.astype(BF)

    scale = 1.0 / math.sqrt(HD)
    image = lax.broadcasted_iota(jnp.int32, (SLOT, 128), 1) // SLOT
    key = lax.broadcasted_iota(jnp.int32, (SLOT, 128), 0)

    def compact(t):
        acc = jnp.where(image == 0, t[0:SLOT], 0.0)
        for i in range(1, 8):
            acc = jnp.where(image == i, t[SLOT * i : SLOT * i + SLOT], acc)
        return acc

    def spread(t):
        return jnp.concatenate([jnp.where(image == i, t, 0.0) for i in range(8)], axis=0)

    def own(h, t):
        low, width = window(h)
        col = lax.broadcasted_iota(jnp.int32, (128, width), 1) + low
        return jnp.where((col >= HD * h) & (col < HD * h + HD), t, jnp.zeros((128, width), BF))

    def head_cols(h, part):
        low, width = window(h)
        return slice(part * W3 + low, part * W3 + low + width)

    def live_rows(b):
        return jnp.broadcast_to(live_v[pl.ds(b, 1), :], (128, 128)).T[:, :1] > 0.5

    def attend(heads, b, _):
        rows = pl.ds(pl.multiple_of(b * 128, 128), 128)
        keys = key < jnp.maximum(jnp.broadcast_to(count_v[pl.ds(b, 1), :], (SLOT, 128)), 1)
        live = live_rows(b)
        for h in heads:
            q = own(h, qkv[rows, head_cols(h, 0)])
            s = jnp.where(keys, compact(dot_nt(qkv[rows, head_cols(h, 1)], q)) * scale, -1e30)
            e = jnp.exp(s - jnp.max(s, axis=0, keepdims=True))
            probs[b, h] = e / jnp.sum(e, axis=0, keepdims=True)
        for h in heads:
            v = own(h, qkv[rows, head_cols(h, 2)])
            o = jnp.where(live, dot_nn(spread(probs[b, h]).T.astype(BF), v), 0.0)
            at = pl.ds(pl.multiple_of(8 * b, 8), 8), slice(None), head_cols(h, 0)
            att[at] += o.astype(BF).reshape(8, SLOT, -1)
        return 0

    def att_start(k, _):
        peer = lax.rem(me + k, NDP)
        for i in range(2):
            lanes[peer, i] = att[inverse_sm[0, 0, 2 * peer + i]]
        remote(lanes.at[peer], arr.at[me], a_sem.at[0], a_sem.at[1], {"dp": peer}).start()
        return 0

    def att_send():
        lax.fori_loop(1, NDP, att_start, 0)
        for i in range(2):
            arr[me, i] = att[inverse_sm[0, 0, 2 * me + i]]

    def take_grad(i, _):
        n = lane_sm[0, 0, i]
        g[i] = garr[n // 2, lax.rem(n, 2)]
        return 0

    def attend_back(heads, b, _):
        rows = pl.ds(pl.multiple_of(b * 128, 128), 128)
        live = live_rows(b)
        for h in heads:
            low, width = window(h)
            q, k, v = (own(h, qkv[rows, head_cols(h, i)]) for i in range(3))
            gh = g[pl.ds(pl.multiple_of(8 * b, 8), 8), :, low : low + width].reshape(128, width)
            gh = jnp.where(live, own(h, gh), jnp.zeros((128, width), BF))
            p = probs[b, h]
            dp = compact(dot_nt(v, gh))
            ds = spread(p * (dp - jnp.sum(dp * p, axis=0, keepdims=True)) * scale)
            dq = dot_nn(ds.T.astype(BF), k)
            dk = dot_nn(ds.astype(BF), q)
            dv = dot_nn(spread(p).astype(BF), gh)
            dqkv[rows, head_cols(h, 0)] += dq.astype(BF)
            dqkv[rows, head_cols(h, 1)] += dk.astype(BF)
            dqkv[rows, head_cols(h, 2)] += dv.astype(BF)
        return 0

    def target(off):
        return lax.rem(z + off + NZ, NZ)

    def weight_grad(h, *offs):
        for off in offs:
            t = target(off)
            left = normed_t[pl.ds(pl.multiple_of(t * SHARD, 32), SHARD), :]
            for low, width in PUT[3 * h : 3 * h + 3]:
                cols = pl.ds(low, width)
                p_all[t, :, :, cols] = dot_nn(left, dqkv[:, cols]).astype(BF).reshape(2, HALF, width)
                src, dst = p_all.at[t, 1 - core, :, cols], pair.at[t, :, cols]
                remote(src, dst, p_send, p_recv.at[h, off + 3], {"dp": sib}).start()

    def pair_wait(h, *offs):
        for off in offs:
            like = pair.at[target(off), :, pl.ds(0, 1152 if h else 768)]
            remote(like, like, p_send, p_recv.at[h, off + 3], {"dp": sib}).wait_recv()

    def ring_valid(d, s, q):
        return s > 0 or (q in (0, 1, 3)) == (d == 0)

    def ring_copy(d, s, q):
        cols = pl.ds(*PUT[q])
        return remote(
            ring_out.at[d, s, :, cols], ring_in.at[d, s, :, cols], r_send, r_recv.at[d, s, q],
            {"fsdp": behind if d else ahead},
        )

    def mine(off, q):
        t = target(off)
        cols = pl.ds(*PUT[q])
        return p_all[t, core, :, cols].astype(F32) + pair[t, :, cols].astype(F32)

    def ring_step(h, s):
        if s == 0:
            pair_wait(h, 4)
        else:
            pair_wait(h, 4 - s, s - 4)
        for q in range(3 * h, 3 * h + 3):
            for d in range(2):
                if not ring_valid(d, s, q):
                    continue
                cols = pl.ds(*PUT[q])
                r = mine(4 if s == 0 else (s - 4 if d else 4 - s), q)
                if s > 0 and ring_valid(d, s - 1, q):
                    ring_copy(d, s - 1, q).wait_recv()
                    r = r + ring_in[d, s - 1, :, cols].astype(F32)
                ring_out[d, s, :, cols] = r.astype(BF)
                ring_copy(d, s, q).start()

    def input_grad(n):
        cols = slice(256 * n, 256 * n + 256)
        for m in range(2):
            dn[256 * m : 256 * m + 256, cols] = dot_nt(dqkv[256 * m : 256 * m + 256, :], wf[cols, :])

    def finish(b, _):
        rows = pl.ds(pl.multiple_of(b * 32, 32), 32)
        x = x_ref[rows, :].astype(F32)
        r = inv[rows, 0:1]
        d = dn[rows, :]
        scaled = d * row[1:2, 0:D]
        m = jnp.mean(scaled * x, axis=-1, keepdims=True)
        dx_ref[rows, :] = (r * scaled - x * (r * r * r) * m).astype(BF)
        t = d * x * r
        dgain[...] += t[0:8] + t[8:16] + t[16:24] + t[24:32]
        return 0

    def bias_sum(b, acc):
        t = dqkv[pl.ds(pl.multiple_of(b * 32, 32), 32), :].astype(F32)
        return acc + (t[0:8] + t[8:16] + t[16:24] + t[24:32])

    dx_out = pltpu.make_async_copy(dx_ref, dx_hbm, l_sem.at[0])

    def small_sums():
        dx_out.start()
        db = jnp.sum(lax.fori_loop(0, 16, bias_sum, jnp.zeros((8, QKV), F32)), axis=0, keepdims=True)
        dg = jnp.sum(dgain[...], axis=0, keepdims=True)
        out = [db[:, 128 * i : 128 * i + 128] for i in range(15)] + [dg[:, 128 * i : 128 * i + 128] for i in range(10)]
        out = jnp.concatenate(out + [jnp.zeros((7, 128), F32)], axis=0)
        sums[...] = out.astype(BF)
        sums_all[z] = out.astype(BF)
        for k in range(1, NZ):
            remote(sums, sums_all.at[z], z_sem.at[0], z_sem.at[1], {"fsdp": lax.rem(z + k, NZ)}).start()

    def scatter(h, i):
        src = tot_small.at[:, pl.ds(0, 384 if h else 256)] if i == PIECES - 1 else tot.at[piece(h, i)]

        @pl.when(chip != i)
        def _():
            remote(src, plane[h].at[chip], x_sem.at[h, 0], x_sem.at[h, 1], {"dp": 2 * i + core}).start()

        @pl.when(chip == i)
        def _():
            plane[h][i] = src[...]

    def ring_end(h):
        pair_wait(h, 0)
        for q in range(3 * h, 3 * h + 3):
            cols = pl.ds(*PUT[q])
            r = mine(0, q)
            for d in range(2):
                ring_copy(d, 3, q).wait_recv()
                r = r + ring_in[d, 3, :, cols].astype(F32)
            tot[:, cols] = r.astype(BF)
            for i in range(5 * (q - 3 * h), 5 * (q - 3 * h) + 5):
                scatter(h, i)

    def plane_sum(h):
        many(plane[h].at[pl.ds(0, CHIPS - 1)], x_sem.at[h]).wait()
        r = plane[h][0].astype(F32)
        for i in range(1, CHIPS):
            r = r + plane[h][i].astype(F32)
        fin[h][core, chip] = r.astype(BF)
        block = fin[h].at[core, chip]

        def share_start(k, _):
            i = lax.rem(chip + k, CHIPS)
            remote(block, block, y_sem.at[h, 0], y_sem.at[h, 1], {"dp": 2 * i + core}).start()
            return 0

        lax.fori_loop(1, CHIPS, share_start, 0)

    def last_copy(h):
        return remote(fin[h].at[core], fin[h].at[core], f_sem.at[h, 0], f_sem.at[h, 1], {"dp": sib})

    def plane_end(h):
        many(fin[h].at[core, pl.ds(0, CHIPS - 1)], y_sem.at[h]).wait()
        last_copy(h).start()

    out_scale = 1.0 / math.sqrt(NDP * NZ * ROWS)

    for s in range(2, 4):
        for h in range(2):
            gather_step(h, s)
    for h in range(2):
        gather_end(h)
        project(h)
    lax.fori_loop(0, 4, functools.partial(attend, range(HEADS)), 0)
    many(garr.at[pl.ds(0, NDP - 1)], g_sem).wait()
    lax.fori_loop(0, IMG, take_grad, 0)
    lax.fori_loop(0, 4, functools.partial(attend_back, range(HEADS)), 0)
    weight_grad(0, 4)
    weight_grad(1, 4)
    weight_grad(0, 3, -3)
    ring_step(0, 0)
    ring_step(1, 0)
    att_send()
    weight_grad(1, 3, -3)
    weight_grad(0, 2, -2)
    weight_grad(1, 2, -2)
    ring_step(0, 1)
    weight_grad(0, 1, -1, 0)
    ring_step(1, 1)
    weight_grad(1, 1, -1, 0)
    input_grad(0)
    input_grad(1)
    ring_step(0, 2)
    input_grad(2)
    input_grad(3)
    ring_step(1, 2)
    input_grad(4)
    lax.fori_loop(0, 8, finish, 0)
    ring_step(0, 3)
    lax.fori_loop(8, 16, finish, 0)
    small_sums()
    ring_step(1, 3)
    ring_end(0)
    many(sums_all.at[pl.ds(0, NZ - 1)], z_sem).wait()
    r = jnp.zeros((32, 128), F32)
    for s in range(NZ):
        r = r + sums_all[s].astype(F32)
    r = [jnp.concatenate([r[3 * i + j : 3 * i + j + 1, :] for j in range(3)], axis=1) for i in range(9)]
    tot_small[...] = jnp.concatenate(r + [jnp.zeros((7, 384), F32)], axis=0).astype(BF)
    scatter(0, PIECES - 1)
    scatter(1, PIECES - 1)
    ring_end(1)
    plane_sum(0)

    many(arr.at[pl.ds(0, NDP - 1)], a_sem).wait()
    slot_copy.wait()

    def place(i, _):
        n = slot_sm[0, 0, i]
        at = jnp.maximum(n, 0)
        block = arr[at // 2, lax.rem(at, 2)]
        out_ref[i] = jnp.where(n >= 0, block, jnp.zeros_like(block))
        return 0

    plane_sum(1)
    plane_end(0)
    lax.fori_loop(0, RECV, place, 0)
    att_out = pltpu.make_async_copy(out_ref, att_hbm, l_sem.at[1])
    att_out.start()
    last_copy(0).wait()
    plane_end(1)
    last_copy(1).wait()
    r = (fin1[0, PIECES - 1].astype(F32) + fin1[1, PIECES - 1].astype(F32)) * out_scale
    for i in range(25):
        part = r[i // 3 : i // 3 + 1, 128 * (i % 3) : 128 * (i % 3) + 128]
        if i < 15:
            row[2:3, 128 * i : 128 * i + 128] = part
        else:
            row[3:4, 128 * (i - 15) : 128 * (i - 15) + 128] = part
    gb = jnp.zeros((1, 240), F32)
    gg = jnp.zeros((1, 160), F32)
    for s in range(NZ):
        gb = jnp.where(z == s, row[2:3, 240 * s : 240 * s + 240], gb)
        gg = jnp.where(z == s, row[3:4, 160 * s : 160 * s + 160], gg)
    gb_ref[...] = gb
    gg_ref[...] = gg

    ring_like = wf.at[pl.ds(0, 560), :]
    pair_like = wf.at[pl.ds(0, 640), :]
    remote(ring_like, ring_like, w_send, w_recv.at[0, 0, 0], {"dp": sib}).wait_send()
    remote(ring_like, ring_like, b_send, b_recv.at[0], {"dp": sib}).wait_send()
    remote(ring_like, ring_like, r_send, r_recv.at[0, 0, 0], {"dp": sib}).wait_send()
    remote(pair_like, pair_like, p_send, p_recv.at[0, 0], {"dp": sib}).wait_send()
    dx_out.wait()
    att_out.wait()


def block(dest, amount, bias, gain, x, weight, grad):
    dma = pltpu.SemaphoreType.DMA
    vmem = pltpu.VMEM
    smem = pltpu.SMEM
    i32 = jnp.int32
    return pl.pallas_call(
        block_kernel,
        out_shape=(
            jax.ShapeDtypeStruct((ROWS, D), BF),
            jax.ShapeDtypeStruct((RECV, SLOT, W3), BF),
            jax.ShapeDtypeStruct((2, CHIPS, SLOT, 256), BF),
            jax.ShapeDtypeStruct((2, CHIPS, SLOT, 384), BF),
            jax.ShapeDtypeStruct((1, 240), F32),
            jax.ShapeDtypeStruct((1, 160), F32),
        ),
        in_specs=[SM, SM, VM, VM, ANY, ANY, ANY],
        out_specs=(ANY, ANY, VM, VM, VM, VM),
        scratch_shapes=[
            vmem((ROWS, D), BF),
            vmem((RECV, SLOT, W3), BF),
            vmem((ROWS, D), BF),
            vmem((RECV, SLOT, W3), BF),
            vmem((D, QKV), BF),
            vmem((8, 256), F32),
            vmem((NZ, 8, 256), F32),
            vmem((1, 1, 128), i32),
            vmem((NDP, 1, 128), i32),
            vmem((NDP, 2, SLOT, W3), BF),
            vmem((NDP, 2, SLOT, W3), BF),
            vmem((3, 1, 128), i32),
            smem((NDP, 1, 128), i32),
            smem((1, 1, 128), i32),
            smem((1, 1, 128), i32),
            smem((1, 1, 128), i32),
            smem((NDP,), i32),
            vmem((ROWS, D), BF),
            vmem((D, ROWS), BF),
            vmem((ROWS, QKV), BF),
            vmem((ROWS, QKV), BF),
            vmem((IMG, SLOT, W3), BF),
            vmem((IMG, SLOT, W3), BF),
            vmem((4, HEADS, SLOT, 128), F32),
            vmem((ROWS, D), F32),
            vmem((ROWS, 128), F32),
            vmem((8, QKV), F32),
            vmem((8, D), F32),
            vmem((8, 128), i32),
            vmem((8, 128), F32),
            vmem((NDP, 2, SLOT, W3), BF),
            vmem((NDP, 2, SLOT, W3), BF),
            vmem((NZ, 2, HALF, QKV), BF),
            vmem((NZ, HALF, QKV), BF),
            vmem((2, 4, HALF, QKV), BF),
            vmem((2, 4, HALF, QKV), BF),
            vmem((HALF, QKV), BF),
            vmem((SLOT, 384), BF),
            vmem((CHIPS, SLOT, 256), BF),
            vmem((CHIPS, SLOT, 384), BF),
            vmem((32, 128), BF),
            vmem((NZ, 32, 128), BF),
            dma((5,)),
            dma((2,)), dma((2,)), dma((2,)), dma((2,)), dma((2,)), dma((2, 2)), dma((2, 2)), dma((2, 2)),
            dma, dma((2, 4, 6)), dma, dma((2,)), dma, dma((2, 8)), dma, dma((2, 4, 6)),
        ],
        compiler_params=pltpu.CompilerParams(vmem_limit_bytes=LIMIT, collective_id=1, has_side_effects=True),
    )(dest, amount, bias, gain, x, weight, grad)


def hand_out_kernel(
    dx_in, att_in, fin0, fin1, gb_in, gg_in, dx_out, att_out, gw_out, gb_out, gg_out, dx, att, sems
):
    steps = []
    for n, (src, mid, dst) in enumerate(((dx_in, dx, dx_out), (att_in, att, att_out))):
        size = src.shape[0] // 4
        for i in range(4):
            part = pl.ds(size * i, size)
            get = pltpu.make_async_copy(src.at[part], mid.at[part], sems.at[0, n, i])
            put = pltpu.make_async_copy(mid.at[part], dst.at[part], sems.at[1, n, i])
            get.start()
            steps.append((get, put))
    gb_out[...] = gb_in[...]
    gg_out[...] = gg_in[...]
    out_scale = 1.0 / math.sqrt(NDP * NZ * ROWS)
    for h, fin in enumerate((fin0, fin1)):
        for c in range(2):
            for i in range(PIECES - 1):
                rows, cols = piece(h, i)
                gw_out[pl.ds(rows.start + HALF * c, SLOT), cols] = fin[c, i].astype(F32) * out_scale
    for get, put in steps:
        get.wait()
        put.start()
    for get, put in steps:
        put.wait()


def hand_out(dx, att, fin0, fin1, gb, gg):
    gw = jax.ShapeDtypeStruct((SHARD, QKV), F32)
    return pl.pallas_call(
        hand_out_kernel,
        out_shape=tuple(jax.ShapeDtypeStruct(a.shape, a.dtype) for a in (dx, att, gw, gb, gg)),
        in_specs=[ANY, ANY, VM, VM, VM, VM],
        out_specs=(ANY, ANY, VM, VM, VM),
        scratch_shapes=[
            pltpu.VMEM(dx.shape, dx.dtype),
            pltpu.VMEM(att.shape, att.dtype),
            pltpu.SemaphoreType.DMA((2, 2, 4)),
        ],
        compiler_params=pltpu.CompilerParams(vmem_limit_bytes=LIMIT),
    )(dx, att, fin0, fin1, gb, gg)


def local(patches, patch_count, destination, qkv_weight, qkv_bias, norm_gain, grad_out):
    dx, att, fin0, fin1, gb, gg = block(
        destination, patch_count, qkv_bias, norm_gain, patches, qkv_weight, grad_out.reshape(RECV, SLOT, W3)
    )
    dx, att, gw, gb, gg = hand_out(dx, att, fin0, fin1, gb, gg)
    return att.reshape(RECV * SLOT, W3), dx, gw, gb.reshape(-1), gg.reshape(-1)


def solution(mesh):
    return jax.shard_map(
        local,
        mesh=mesh,
        in_specs=(
            P(("dp", "fsdp"), None),
            P(("dp", "fsdp")),
            P(("dp", "fsdp")),
            P("fsdp", None),
            P("fsdp"),
            P("fsdp"),
            P(("dp", "fsdp"), None),
        ),
        out_specs=(
            P(("dp", "fsdp"), None),
            P(("dp", "fsdp"), None),
            P("fsdp", None),
            P("fsdp"),
            P("fsdp"),
        ),
        check_vma=False,
    )
```

```python
import functools
import math

import jax
import jax.numpy as jnp
from jax import lax
from jax.experimental import pallas as pl
from jax.experimental.pallas import tpu as pltpu
from jax.sharding import PartitionSpec as P

MESH = pl.DeviceIdType.MESH
BF = jnp.bfloat16
F32 = jnp.float32
D = 1280
QKV = 1920
HEADS = 8
HD = 80
W3 = HEADS * HD
SLOT = 16
IMG = 32
ROWS = IMG * SLOT
RECV = 56
NDP = 32
NZ = 8
CHIPS = 16
SHARD = D // NZ
HALF = SHARD // 2
PIECES = 16
LIMIT = 58 * 2**20
GET = ((0, 384), (640, 384), (1280, 384), (384, 256), (1024, 256), (1664, 256))
PUT = ((0, 256), (640, 256), (1280, 256), (256, 384), (896, 384), (1536, 384))
ORDER = (4, 3, -3, 2, -2, 1, -1, 0)
VM = pl.BlockSpec(memory_space=pltpu.VMEM)
SM = pl.BlockSpec(memory_space=pltpu.SMEM)
ANY = pl.BlockSpec(memory_space=pl.ANY)


def remote(src, dst, send, recv, where):
    return pltpu.make_async_remote_copy(
        src_ref=src, dst_ref=dst, send_sem=send, recv_sem=recv, device_id=where, device_id_type=MESH
    )


def dot_nn(a, b):
    return lax.dot_general(a, b, (((1,), (0,)), ((), ())), preferred_element_type=F32)


def dot_nt(a, b):
    return lax.dot_general(a, b, (((1,), (1,)), ((), ())), preferred_element_type=F32)


def window(h):
    low = (HD * h // 128) * 128
    high = -(-(HD * h + HD) // 128) * 128
    return low, high - low


def piece(h, i):
    return pl.ds(SLOT * (i % 5), SLOT), pl.ds(*PUT[3 * h + i // 5])


def block_kernel(
    dest_ref, amount_ref, bias_ref, gain_ref, x_hbm, w_hbm, grad_hbm,
    dx_hbm, att_hbm, fin0, fin1, gb_ref, gg_ref,
    x_ref, grad_ref, dx_ref, out_ref,
    wf, small_ref, small_all, cmine, cbuf, stage, garr, tabs, csm, lane_sm, inverse_sm, slot_sm, starts,
    normed, normed_t, qkv, dqkv, g, att, probs, dn, inv, row, dgain, count_v, live_v,
    lanes, arr, p_all, pair, ring_in, ring_out, tot, tot_small, plane0, plane1, sums, sums_all,
    l_sem, c_sem, g_sem, s_sem, a_sem, z_sem, x_sem, y_sem, f_sem, w_send, w_recv, b_send, b_recv,
    p_send, p_recv, r_send, r_recv,
):
    me = lax.axis_index("dp")
    z = lax.axis_index("fsdp")
    core = lax.rem(me, 2)
    chip = me // 2
    sib = me + 1 - 2 * core
    ahead, behind = lax.rem(z + 1, NZ), lax.rem(z + NZ - 1, NZ)
    plane, fin = (plane0, plane1), (fin0, fin1)

    def many(like, sems):
        return remote(like, like, sems.at[0], sems.at[1], {"dp": sib})

    x_in = pltpu.make_async_copy(x_hbm, x_ref, l_sem.at[0])
    w_in = pltpu.make_async_copy(w_hbm, wf.at[pl.ds(pl.multiple_of(z * SHARD, 32), SHARD), :], l_sem.at[1])
    grad_in = pltpu.make_async_copy(grad_hbm, grad_ref, l_sem.at[2])
    w_in.start()
    grad_in.start()
    x_in.start()

    barrier = pltpu.get_barrier_semaphore()

    def greet(k, _):
        pl.semaphore_signal(barrier, inc=1, device_id={"dp": lax.rem(me + k, NDP)}, device_id_type=MESH)
        return 0

    lax.fori_loop(1, NDP, greet, 0)
    for k in range(1, NZ):
        pl.semaphore_signal(barrier, inc=1, device_id={"fsdp": lax.rem(z + k, NZ)}, device_id_type=MESH)

    lane = lax.broadcasted_iota(jnp.int32, (1, 128), 1)
    dests = [dest_ref[i] for i in range(IMG)]
    per = jnp.zeros((1, 128), jnp.int32)
    to = jnp.zeros((1, 128), jnp.int32)
    for i in range(IMG):
        per = per + jnp.where(lane == dests[i], 1, 0)
        to = jnp.where(lane == i, dests[i], to)
    cmine[0] = per
    cbuf[me] = per
    rank = jnp.zeros((1, 128), jnp.int32)
    for i in range(IMG):
        rank = rank + jnp.where((to == dests[i]) & (lane > i), 1, 0)
    tabs[0] = 2 * to + jnp.minimum(rank, 1)
    lane_copy = pltpu.make_async_copy(tabs.at[pl.ds(0, 1)], lane_sm, l_sem.at[3])
    lane_copy.start()
    lane_copy.wait()
    source = jnp.zeros((1, 128), jnp.int32)
    for i in range(IMG):
        source = jnp.where(lane == lane_sm[0, 0, i], i, source)
    tabs[1] = source
    inverse_copy = pltpu.make_async_copy(tabs.at[pl.ds(1, 1)], inverse_sm, l_sem.at[4])
    inverse_copy.start()
    for b in range(4):
        have = jnp.zeros((1, 128), jnp.int32)
        for i in range(8):
            have = jnp.where(lane // SLOT == i, amount_ref[8 * b + i], have)
        count_v[b : b + 1, :] = have
        live_v[b : b + 1, :] = jnp.where(lax.rem(lane, SLOT) < have, 1.0, 0.0)
    small_ref[0:1, 0:240] = bias_ref[...].astype(F32).reshape(1, 240)
    small_ref[1:2, 0:160] = gain_ref[...].astype(F32).reshape(1, 160)
    small_all[z] = small_ref[...]
    w_in.wait()
    pl.semaphore_wait(barrier, NDP - 1 + NZ - 1)

    def rows_of(t):
        return pl.ds(pl.multiple_of(t * SHARD + core * HALF, 16), HALF)

    def gather_valid(d, s, q):
        return s < 3 or (s == 3 and (q in (0, 1, 3)) == (d == 0))

    def got_shard(d, s):
        return lax.rem(z - 1 - s + NZ, NZ) if d == 0 else lax.rem(z + 1 + s, NZ)

    def gather_copy(d, s, q):
        block = wf.at[rows_of(got_shard(d, s - 1)), pl.ds(*GET[q])]
        return remote(block, block, w_send, w_recv.at[d, s, q], {"fsdp": behind if d else ahead})

    def gather_start(h):
        for q in range(3 * h, 3 * h + 3):
            for d in range(2):
                gather_copy(d, 0, q).start()

    def gather_step(h, s):
        for q in range(3 * h, 3 * h + 3):
            for d in range(2):
                if not gather_valid(d, s, q):
                    continue
                gather_copy(d, s, q).wait_recv()
                if gather_valid(d, s + 1, q):
                    gather_copy(d, s + 1, q).start()
                block = wf.at[rows_of(got_shard(d, s)), pl.ds(*GET[q])]
                remote(block, block, b_send, b_recv.at[h], {"dp": sib}).start()

    def gather_end(h):
        like = wf.at[pl.ds(0, 7 * HALF), pl.ds(0, 768 if h else 1152)]
        remote(like, like, b_send, b_recv.at[h], {"dp": sib}).wait_recv()

    def count_start(k, _):
        remote(cmine.at[0], cbuf.at[me], c_sem.at[0], c_sem.at[1], {"dp": lax.rem(me + k, NDP)}).start()
        return 0

    gather_start(0)
    gather_start(1)
    lax.fori_loop(1, NDP, count_start, 0)

    for k in range(1, NZ):
        remote(small_ref, small_all.at[z], s_sem.at[0], s_sem.at[1], {"fsdp": lax.rem(z + k, NZ)}).start()

    many(cbuf.at[pl.ds(0, NDP - 1)], c_sem).wait()
    to_smem = pltpu.make_async_copy(cbuf, csm, l_sem.at[3])
    to_smem.start()
    to_smem.wait()

    def prefix(s, carry):
        start, table = carry
        n = csm[s, 0, me]
        starts[s] = start
        table = jnp.where((lane >= start) & (lane < start + n), 2 * s + lane - start, table)
        return start + n, table

    _, table = lax.fori_loop(0, NDP, prefix, (jnp.int32(0), jnp.full((1, 128), -1, jnp.int32)))
    tabs[2] = table
    inverse_copy.wait()
    slot_copy = pltpu.make_async_copy(tabs.at[pl.ds(2, 1)], slot_sm, l_sem.at[4])
    slot_copy.start()

    def pick_grad(peer):
        first = jnp.minimum(starts[peer], RECV - 1)
        return grad_ref[first], grad_ref[jnp.minimum(first + 1, RECV - 1)]

    def grad_start(k, _):
        peer = lax.rem(me + k, NDP)
        stage[peer, 0], stage[peer, 1] = pick_grad(peer)
        remote(stage.at[peer], garr.at[me], g_sem.at[0], g_sem.at[1], {"dp": peer}).start()
        return 0

    grad_in.wait()
    gather_step(0, 0)
    gather_step(1, 0)
    lax.fori_loop(1, 16, grad_start, 0)
    gather_step(0, 1)
    gather_step(1, 1)
    lax.fori_loop(16, NDP, grad_start, 0)
    garr[me, 0], garr[me, 1] = pick_grad(me)

    many(small_all.at[pl.ds(0, NZ - 1)], s_sem).wait()
    for s in range(NZ):
        row[0:1, 240 * s : 240 * s + 240] = small_all[s, 0:1, 0:240]
        row[1:2, 160 * s : 160 * s + 160] = small_all[s, 1:2, 0:160]
    x_in.wait()

    def norm_block(b, _):
        rows = pl.ds(pl.multiple_of(b * 128, 128), 128)
        x = x_ref[rows, :].astype(F32)
        r = lax.rsqrt(jnp.mean(x * x, axis=-1, keepdims=True) + 1e-06)
        inv[rows, :] = jnp.broadcast_to(r, (128, 128))
        y = x * r * row[1:2, 0:D]
        normed[rows, :] = y.astype(BF)
        normed_t[:, rows] = y.T.astype(BF)
        return 0

    lax.fori_loop(0, 4, norm_block, 0)
    dqkv[...] = jnp.zeros_like(dqkv)
    att[...] = jnp.zeros_like(att)
    dgain[...] = jnp.zeros_like(dgain)

    def project(h):
        for low, width in GET[3 * h : 3 * h + 3]:
            for m in range(2):
                r = dot_nn(normed[256 * m : 256 * m + 256, :], wf[:, low : low + width]) + row[0:1, low : low + width]
                qkv[256 * m : 256 * m + 256, low : low + width] = r.astype(BF)

    scale = 1.0 / math.sqrt(HD)
    image = lax.broadcasted_iota(jnp.int32, (SLOT, 128), 1) // SLOT
    key = lax.broadcasted_iota(jnp.int32, (SLOT, 128), 0)

    def compact(t):
        acc = jnp.where(image == 0, t[0:SLOT], 0.0)
        for i in range(1, 8):
            acc = jnp.where(image == i, t[SLOT * i : SLOT * i + SLOT], acc)
        return acc

    def spread(t):
        return jnp.concatenate([jnp.where(image == i, t, 0.0) for i in range(8)], axis=0)

    def own(h, t):
        low, width = window(h)
        col = lax.broadcasted_iota(jnp.int32, (128, width), 1) + low
        return jnp.where((col >= HD * h) & (col < HD * h + HD), t, jnp.zeros((128, width), BF))

    def head_cols(h, part):
        low, width = window(h)
        return slice(part * W3 + low, part * W3 + low + width)

    def live_rows(b):
        return jnp.broadcast_to(live_v[pl.ds(b, 1), :], (128, 128)).T[:, :1] > 0.5

    def attend(heads, b, _):
        rows = pl.ds(pl.multiple_of(b * 128, 128), 128)
        keys = key < jnp.maximum(jnp.broadcast_to(count_v[pl.ds(b, 1), :], (SLOT, 128)), 1)
        live = live_rows(b)
        for h in heads:
            q = own(h, qkv[rows, head_cols(h, 0)])
            s = jnp.where(keys, compact(dot_nt(qkv[rows, head_cols(h, 1)], q)) * scale, -1e30)
            e = jnp.exp(s - jnp.max(s, axis=0, keepdims=True))
            probs[b, h] = e / jnp.sum(e, axis=0, keepdims=True)
        for h in heads:
            v = own(h, qkv[rows, head_cols(h, 2)])
            o = jnp.where(live, dot_nn(spread(probs[b, h]).astype(BF).T, v), 0.0)
            at = pl.ds(pl.multiple_of(8 * b, 8), 8), slice(None), head_cols(h, 0)
            att[at] += o.astype(BF).reshape(8, SLOT, -1)
        return 0

    def att_start(k, _):
        peer = lax.rem(me + k, NDP)
        for i in range(2):
            lanes[peer, i] = att[inverse_sm[0, 0, 2 * peer + i]]
        remote(lanes.at[peer], arr.at[me], a_sem.at[0], a_sem.at[1], {"dp": peer}).start()
        return 0

    def att_send():
        lax.fori_loop(1, NDP, att_start, 0)
        for i in range(2):
            arr[me, i] = att[inverse_sm[0, 0, 2 * me + i]]

    def take_grad(i, _):
        n = lane_sm[0, 0, i]
        g[i] = garr[n // 2, lax.rem(n, 2)]
        return 0

    def attend_back(heads, b, _):
        rows = pl.ds(pl.multiple_of(b * 128, 128), 128)
        live = live_rows(b)
        for h in heads:
            low, width = window(h)
            q, k, v = (own(h, qkv[rows, head_cols(h, i)]) for i in range(3))
            gh = g[pl.ds(pl.multiple_of(8 * b, 8), 8), :, low : low + width].reshape(128, width)
            gh = jnp.where(live, own(h, gh), jnp.zeros((128, width), BF))
            p = probs[b, h]
            dp = compact(dot_nt(v, gh))
            ds = spread(p * (dp - jnp.sum(dp * p, axis=0, keepdims=True)) * scale).astype(BF)
            dq = dot_nn(ds.T, k)
            dk = dot_nn(ds, q)
            dv = dot_nn(spread(p).astype(BF), gh)
            dqkv[rows, head_cols(h, 0)] += dq.astype(BF)
            dqkv[rows, head_cols(h, 1)] += dk.astype(BF)
            dqkv[rows, head_cols(h, 2)] += dv.astype(BF)
        return 0

    def target(off):
        return lax.rem(z + off + NZ, NZ)

    def weight_grad(h, *offs):
        for off in offs:
            t = target(off)
            left = normed_t[pl.ds(pl.multiple_of(t * SHARD, 32), SHARD), :]
            for low, width in PUT[3 * h : 3 * h + 3]:
                cols = pl.ds(low, width)
                p_all[t, :, :, cols] = dot_nn(left, dqkv[:, cols]).astype(BF).reshape(2, HALF, width)
                src, dst = p_all.at[t, 1 - core, :, cols], pair.at[t, :, cols]
                remote(src, dst, p_send, p_recv.at[h, off + 3], {"dp": sib}).start()

    def pair_wait(h, *offs):
        for off in offs:
            like = pair.at[target(off), :, pl.ds(0, 1152 if h else 768)]
            remote(like, like, p_send, p_recv.at[h, off + 3], {"dp": sib}).wait_recv()

    def ring_valid(d, s, q):
        return s > 0 or (q in (0, 1, 3)) == (d == 0)

    def ring_copy(d, s, q):
        cols = pl.ds(*PUT[q])
        return remote(
            ring_out.at[d, s, :, cols], ring_in.at[d, s, :, cols], r_send, r_recv.at[d, s, q],
            {"fsdp": behind if d else ahead},
        )

    def mine(off, q):
        t = target(off)
        cols = pl.ds(*PUT[q])
        return p_all[t, core, :, cols].astype(F32) + pair[t, :, cols].astype(F32)

    def ring_step(h, s):
        if s == 0:
            pair_wait(h, 4)
        else:
            pair_wait(h, 4 - s, s - 4)
        for q in range(3 * h, 3 * h + 3):
            for d in range(2):
                if not ring_valid(d, s, q):
                    continue
                cols = pl.ds(*PUT[q])
                r = mine(4 if s == 0 else (s - 4 if d else 4 - s), q)
                if s > 0 and ring_valid(d, s - 1, q):
                    ring_copy(d, s - 1, q).wait_recv()
                    r = r + ring_in[d, s - 1, :, cols].astype(F32)
                ring_out[d, s, :, cols] = r.astype(BF)
                ring_copy(d, s, q).start()

    def input_grad(n):
        cols = slice(256 * n, 256 * n + 256)
        for m in range(2):
            dn[256 * m : 256 * m + 256, cols] = dot_nt(dqkv[256 * m : 256 * m + 256, :], wf[cols, :])

    def finish(b, _):
        rows = pl.ds(pl.multiple_of(b * 32, 32), 32)
        x = x_ref[rows, :].astype(F32)
        r = inv[rows, 0:1]
        d = dn[rows, :]
        scaled = d * row[1:2, 0:D]
        m = jnp.mean(scaled * x, axis=-1, keepdims=True)
        dx_ref[rows, :] = (r * scaled - x * (r * r * r) * m).astype(BF)
        t = d * x * r
        dgain[...] += t[0:8] + t[8:16] + t[16:24] + t[24:32]
        return 0

    def bias_sum(b, acc):
        t = dqkv[pl.ds(pl.multiple_of(b * 32, 32), 32), :].astype(F32)
        return acc + (t[0:8] + t[8:16] + t[16:24] + t[24:32])

    dx_out = pltpu.make_async_copy(dx_ref, dx_hbm, l_sem.at[0])

    def small_sums():
        dx_out.start()
        db = jnp.sum(lax.fori_loop(0, 16, bias_sum, jnp.zeros((8, QKV), F32)), axis=0, keepdims=True)
        dg = jnp.sum(dgain[...], axis=0, keepdims=True)
        out = [db[:, 128 * i : 128 * i + 128] for i in range(15)] + [dg[:, 128 * i : 128 * i + 128] for i in range(10)]
        out = jnp.concatenate(out + [jnp.zeros((7, 128), F32)], axis=0)
        sums[...] = out.astype(BF)
        sums_all[z] = out.astype(BF)
        for k in range(1, NZ):
            remote(sums, sums_all.at[z], z_sem.at[0], z_sem.at[1], {"fsdp": lax.rem(z + k, NZ)}).start()

    def scatter(h, i):
        src = tot_small.at[:, pl.ds(0, 384 if h else 256)] if i == PIECES - 1 else tot.at[piece(h, i)]

        @pl.when(chip != i)
        def _():
            remote(src, plane[h].at[chip], x_sem.at[h, 0], x_sem.at[h, 1], {"dp": 2 * i + core}).start()

        @pl.when(chip == i)
        def _():
            plane[h][i] = src[...]

    def ring_end(h):
        pair_wait(h, 0)
        for q in range(3 * h, 3 * h + 3):
            cols = pl.ds(*PUT[q])
            r = mine(0, q)
            for d in range(2):
                ring_copy(d, 3, q).wait_recv()
                r = r + ring_in[d, 3, :, cols].astype(F32)
            tot[:, cols] = r.astype(BF)
            for i in range(5 * (q - 3 * h), 5 * (q - 3 * h) + 5):
                scatter(h, i)

    def plane_sum(h):
        many(plane[h].at[pl.ds(0, CHIPS - 1)], x_sem.at[h]).wait()
        r = plane[h][0].astype(F32)
        for i in range(1, CHIPS):
            r = r + plane[h][i].astype(F32)
        fin[h][core, chip] = r.astype(BF)
        block = fin[h].at[core, chip]

        def share_start(k, _):
            i = lax.rem(chip + k, CHIPS)
            remote(block, block, y_sem.at[h, 0], y_sem.at[h, 1], {"dp": 2 * i + core}).start()
            return 0

        lax.fori_loop(1, CHIPS, share_start, 0)

    def last_copy(h):
        return remote(fin[h].at[core], fin[h].at[core], f_sem.at[h, 0], f_sem.at[h, 1], {"dp": sib})

    def plane_end(h):
        many(fin[h].at[core, pl.ds(0, CHIPS - 1)], y_sem.at[h]).wait()
        last_copy(h).start()

    out_scale = 1.0 / math.sqrt(NDP * NZ * ROWS)

    for s in range(2, 4):
        for h in range(2):
            gather_step(h, s)
    for h in range(2):
        gather_end(h)
        project(h)
    lax.fori_loop(0, 4, functools.partial(attend, range(HEADS)), 0)
    many(garr.at[pl.ds(0, NDP - 1)], g_sem).wait()
    lax.fori_loop(0, IMG, take_grad, 0)
    lax.fori_loop(0, 4, functools.partial(attend_back, range(HEADS)), 0)
    weight_grad(0, 4)
    weight_grad(1, 4)
    weight_grad(0, 3, -3)
    ring_step(0, 0)
    ring_step(1, 0)
    att_send()
    weight_grad(1, 3, -3)
    weight_grad(0, 2, -2)
    weight_grad(1, 2, -2)
    ring_step(0, 1)
    weight_grad(0, 1, -1, 0)
    ring_step(1, 1)
    weight_grad(1, 1, -1, 0)
    for n in range(3):
        input_grad(n)
    ring_step(0, 2)
    input_grad(3)
    ring_step(1, 2)
    input_grad(4)
    lax.fori_loop(0, 16, finish, 0)
    small_sums()
    ring_step(0, 3)
    ring_step(1, 3)
    ring_end(0)
    many(sums_all.at[pl.ds(0, NZ - 1)], z_sem).wait()
    r = jnp.zeros((32, 128), F32)
    for s in range(NZ):
        r = r + sums_all[s].astype(F32)
    r = [jnp.concatenate([r[3 * i + j : 3 * i + j + 1, :] for j in range(3)], axis=1) for i in range(9)]
    tot_small[...] = jnp.concatenate(r + [jnp.zeros((7, 384), F32)], axis=0).astype(BF)
    scatter(0, PIECES - 1)
    scatter(1, PIECES - 1)
    ring_end(1)
    plane_sum(0)


    def place(i, _):
        n = slot_sm[0, 0, i]
        at = jnp.maximum(n, 0)
        block = arr[at // 2, lax.rem(at, 2)]
        out_ref[i] = jnp.where(n >= 0, block, jnp.zeros_like(block))
        return 0

    plane_sum(1)
    plane_end(0)
    many(arr.at[pl.ds(0, NDP - 1)], a_sem).wait()
    slot_copy.wait()
    lax.fori_loop(0, RECV, place, 0)
    att_out = pltpu.make_async_copy(out_ref, att_hbm, l_sem.at[1])
    att_out.start()
    last_copy(0).wait()
    plane_end(1)
    last_copy(1).wait()
    r = (fin1[0, PIECES - 1].astype(F32) + fin1[1, PIECES - 1].astype(F32)) * out_scale
    for i in range(25):
        part = r[i // 3 : i // 3 + 1, 128 * (i % 3) : 128 * (i % 3) + 128]
        if i < 15:
            row[2:3, 128 * i : 128 * i + 128] = part
        else:
            row[3:4, 128 * (i - 15) : 128 * (i - 15) + 128] = part
    gb = jnp.zeros((1, 240), F32)
    gg = jnp.zeros((1, 160), F32)
    for s in range(NZ):
        gb = jnp.where(z == s, row[2:3, 240 * s : 240 * s + 240], gb)
        gg = jnp.where(z == s, row[3:4, 160 * s : 160 * s + 160], gg)
    gb_ref[...] = gb
    gg_ref[...] = gg

    ring_like = wf.at[pl.ds(0, 560), :]
    pair_like = wf.at[pl.ds(0, 640), :]
    remote(ring_like, ring_like, w_send, w_recv.at[0, 0, 0], {"dp": sib}).wait_send()
    remote(ring_like, ring_like, b_send, b_recv.at[0], {"dp": sib}).wait_send()
    remote(ring_like, ring_like, r_send, r_recv.at[0, 0, 0], {"dp": sib}).wait_send()
    remote(pair_like, pair_like, p_send, p_recv.at[0, 0], {"dp": sib}).wait_send()
    dx_out.wait()
    att_out.wait()


def block(dest, amount, bias, gain, x, weight, grad):
    dma = pltpu.SemaphoreType.DMA
    vmem = pltpu.VMEM
    smem = pltpu.SMEM
    i32 = jnp.int32
    return pl.pallas_call(
        block_kernel,
        out_shape=(
            jax.ShapeDtypeStruct((ROWS, D), BF),
            jax.ShapeDtypeStruct((RECV, SLOT, W3), BF),
            jax.ShapeDtypeStruct((2, CHIPS, SLOT, 256), BF),
            jax.ShapeDtypeStruct((2, CHIPS, SLOT, 384), BF),
            jax.ShapeDtypeStruct((1, 240), F32),
            jax.ShapeDtypeStruct((1, 160), F32),
        ),
        in_specs=[SM, SM, VM, VM, ANY, ANY, ANY],
        out_specs=(ANY, ANY, VM, VM, VM, VM),
        scratch_shapes=[
            vmem((ROWS, D), BF),
            vmem((RECV, SLOT, W3), BF),
            vmem((ROWS, D), BF),
            vmem((RECV, SLOT, W3), BF),
            vmem((D, QKV), BF),
            vmem((8, 256), F32),
            vmem((NZ, 8, 256), F32),
            vmem((1, 1, 128), i32),
            vmem((NDP, 1, 128), i32),
            vmem((NDP, 2, SLOT, W3), BF),
            vmem((NDP, 2, SLOT, W3), BF),
            vmem((3, 1, 128), i32),
            smem((NDP, 1, 128), i32),
            smem((1, 1, 128), i32),
            smem((1, 1, 128), i32),
            smem((1, 1, 128), i32),
            smem((NDP,), i32),
            vmem((ROWS, D), BF),
            vmem((D, ROWS), BF),
            vmem((ROWS, QKV), BF),
            vmem((ROWS, QKV), BF),
            vmem((IMG, SLOT, W3), BF),
            vmem((IMG, SLOT, W3), BF),
            vmem((4, HEADS, SLOT, 128), F32),
            vmem((ROWS, D), F32),
            vmem((ROWS, 128), F32),
            vmem((8, QKV), F32),
            vmem((8, D), F32),
            vmem((8, 128), i32),
            vmem((8, 128), F32),
            vmem((NDP, 2, SLOT, W3), BF),
            vmem((NDP, 2, SLOT, W3), BF),
            vmem((NZ, 2, HALF, QKV), BF),
            vmem((NZ, HALF, QKV), BF),
            vmem((2, 4, HALF, QKV), BF),
            vmem((2, 4, HALF, QKV), BF),
            vmem((HALF, QKV), BF),
            vmem((SLOT, 384), BF),
            vmem((CHIPS, SLOT, 256), BF),
            vmem((CHIPS, SLOT, 384), BF),
            vmem((32, 128), BF),
            vmem((NZ, 32, 128), BF),
            dma((5,)),
            dma((2,)), dma((2,)), dma((2,)), dma((2,)), dma((2,)), dma((2, 2)), dma((2, 2)), dma((2, 2)),
            dma, dma((2, 4, 6)), dma, dma((2,)), dma, dma((2, 8)), dma, dma((2, 4, 6)),
        ],
        compiler_params=pltpu.CompilerParams(vmem_limit_bytes=LIMIT, collective_id=1, has_side_effects=True),
    )(dest, amount, bias, gain, x, weight, grad)


def hand_out_kernel(
    dx_in, att_in, fin0, fin1, gb_in, gg_in, dx_out, att_out, gw_out, gb_out, gg_out, dx, att, sems
):
    steps = []
    for n, (src, mid, dst) in enumerate(((dx_in, dx, dx_out), (att_in, att, att_out))):
        size = src.shape[0] // 4
        for i in range(4):
            part = pl.ds(size * i, size)
            get = pltpu.make_async_copy(src.at[part], mid.at[part], sems.at[0, n, i])
            put = pltpu.make_async_copy(mid.at[part], dst.at[part], sems.at[1, n, i])
            get.start()
            steps.append((get, put))
    gb_out[...] = gb_in[...]
    gg_out[...] = gg_in[...]
    out_scale = 1.0 / math.sqrt(NDP * NZ * ROWS)
    for h, fin in enumerate((fin0, fin1)):
        for c in range(2):
            for i in range(PIECES - 1):
                rows, cols = piece(h, i)
                gw_out[pl.ds(rows.start + HALF * c, SLOT), cols] = fin[c, i].astype(F32) * out_scale
    for get, put in steps:
        get.wait()
        put.start()
    for get, put in steps:
        put.wait()


def hand_out(dx, att, fin0, fin1, gb, gg):
    gw = jax.ShapeDtypeStruct((SHARD, QKV), F32)
    return pl.pallas_call(
        hand_out_kernel,
        out_shape=tuple(jax.ShapeDtypeStruct(a.shape, a.dtype) for a in (dx, att, gw, gb, gg)),
        in_specs=[ANY, ANY, VM, VM, VM, VM],
        out_specs=(ANY, ANY, VM, VM, VM),
        scratch_shapes=[
            pltpu.VMEM(dx.shape, dx.dtype),
            pltpu.VMEM(att.shape, att.dtype),
            pltpu.SemaphoreType.DMA((2, 2, 4)),
        ],
        compiler_params=pltpu.CompilerParams(vmem_limit_bytes=LIMIT),
    )(dx, att, fin0, fin1, gb, gg)


def local(patches, patch_count, destination, qkv_weight, qkv_bias, norm_gain, grad_out):
    dx, att, fin0, fin1, gb, gg = block(
        destination, patch_count, qkv_bias, norm_gain, patches, qkv_weight, grad_out.reshape(RECV, SLOT, W3)
    )
    dx, att, gw, gb, gg = hand_out(dx, att, fin0, fin1, gb, gg)
    return att.reshape(RECV * SLOT, W3), dx, gw, gb.reshape(-1), gg.reshape(-1)


def solution(mesh):
    return jax.shard_map(
        local,
        mesh=mesh,
        in_specs=(
            P(("dp", "fsdp"), None),
            P(("dp", "fsdp")),
            P(("dp", "fsdp")),
            P("fsdp", None),
            P("fsdp"),
            P("fsdp"),
            P(("dp", "fsdp"), None),
        ),
        out_specs=(
            P(("dp", "fsdp"), None),
            P(("dp", "fsdp"), None),
            P("fsdp", None),
            P("fsdp"),
            P("fsdp"),
        ),
        check_vma=False,
    )
```
